32 devices in a mesh: dp: 8 (over z, y), col: 4 (over x, core).
Axes of the slice: x: 2, y: 2, z: 4, core: 2. Of those that a mesh axis runs over, the one named last changes fastest.
Arguments:
- tokens: bfloat16 [32768, 1024], P(('dp', 'col')), may hold values from -6 to 6
- cotangent: bfloat16 [32768, 1024], P(('dp', 'col')), may hold values from -6 to 6
- ln1_gain: bfloat16 [1024], replicated, may hold values from 0.5 to 1.5
- ln1_shift: bfloat16 [1024], replicated, may hold values from -1.5 to 1.5
- qkv_weight: bfloat16 [1024, 3072], replicated, may hold values from -0.1875 to 0.1875
- qkv_bias: bfloat16 [3072], replicated, may hold values from -1.5 to 1.5
- out_weight: bfloat16 [1024, 1024], replicated, may hold values from -0.75 to 0.75
- out_bias: bfloat16 [1024], replicated, may hold values from -1.5 to 1.5
- ln2_gain: bfloat16 [1024], replicated, may hold values from 0.5 to 1.5
- ln2_shift: bfloat16 [1024], replicated, may hold values from -1.5 to 1.5
- fc_weight: bfloat16 [1024, 4096], replicated, may hold values from -0.1875 to 0.1875
- fc_bias: bfloat16 [4096], replicated, may hold values from -1.5 to 1.5
- proj_weight: bfloat16 [4096, 1024], replicated, may hold values from -0.09375 to 0.09375
- proj_bias: bfloat16 [1024], replicated, may hold values from -1.5 to 1.5
- embedding: bfloat16 [10, 1024], replicated, may hold values from -6 to 6
- first_weight: bfloat16 [1024, 512], replicated, may hold values from -0.1875 to 0.1875
- first_bias: bfloat16 [512], replicated, may hold values from -1.5 to 1.5
- second_weight: bfloat16 [512, 2048], P(None, 'col'), may hold values from -0.25 to 0.25
- second_bias: bfloat16 [2048], P('col'), may hold values from -1.5 to 1.5
Outputs:
- block_out: bfloat16 [32768, 1024], P(('dp', 'col'))
- token_grad: bfloat16 [32768, 1024], P(('dp', 'col'))
- embed_grad: float32 [10, 1024], replicated
- first_grad: float32 [1024, 512], replicated
- first_bias_grad: float32 [512], replicated
- second_grad: float32 [512, 2048], P(None, 'col')
- second_bias_grad: float32 [2048], P('col')
The draws below stay inside these ranges and needn't reach their ends.
All inputs are finite; a program needn't handle non-finite values.
Results may differ from the reference program's by a relative error of at most 0.013.
Values may be sent and summed in bfloat16 or wider, within the bound.
A program may use at most 192 MiB of HBM per device.

```python
import math
import jax
import jax.numpy as jnp
from jax import lax

D = 1024
HEADS = 16
FF = 4096
PREFIX = 10
RHID = 512
KV_COLS = 2048
SEQ_LEN = 256
SEQS = 128
TOKENS = 32768


def shard_levels(stream_key, extent, cuts, low, high):
    level, own = 1.0, jax.random.fold_in(stream_key, 6)
    for axis_at, parts in cuts:
        draws = jnp.exp(jax.random.uniform(jax.random.fold_in(own, axis_at), (parts,), jnp.float32, low / len(cuts), high / len(cuts)))
        level = level * jnp.repeat(draws, extent[axis_at] // parts).reshape([-1 if axis == axis_at else 1 for axis in range(len(extent))])
    return level


def noise(key, dims, deviation, reach, split=(), kind=jnp.bfloat16):
    array = jax.random.normal(key, dims, jnp.float32) * deviation
    if len(split) > 0:
        array = shard_levels(key, dims, split, -0.22, 0.18) * array
    return jnp.clip(array, min=-reach, max=reach).astype(kind)


def setup_inputs(seed: int = 0) -> dict:
    splits = jax.random.split(jax.random.key(seed), 20)
    return {
        "tokens": noise(splits[0], (TOKENS, D), 1.0, 6.0, ((0, 32),)),
        "cotangent": noise(splits[1], (TOKENS, D), 1.0, 6.0, ((0, 32),)),
        "ln1_gain": jnp.clip(1.0 + 0.1 * jax.random.normal(splits[2], (D,), jnp.float32), 0.5, 1.5).astype(jnp.bfloat16),
        "ln1_shift": noise(splits[3], (D,), 0.3, 1.5),
        "qkv_weight": noise(splits[4], (D, 3 * D), D ** -0.5, 0.1875),
        "qkv_bias": noise(splits[5], (3 * D,), 0.3, 1.5),
        "out_weight": noise(splits[6], (D, D), (D // 16) ** -0.5, 0.75),
        "out_bias": noise(splits[7], (D,), 0.3, 1.5),
        "ln2_gain": jnp.clip(1.0 + 0.1 * jax.random.normal(splits[8], (D,), jnp.float32), 0.5, 1.5).astype(jnp.bfloat16),
        "ln2_shift": noise(splits[9], (D,), 0.3, 1.5),
        "fc_weight": noise(splits[10], (D, FF), D ** -0.5, 0.1875),
        "fc_bias": noise(splits[11], (FF,), 0.3, 1.5),
        "proj_weight": noise(splits[12], (FF, D), FF ** -0.5, 0.09375),
        "proj_bias": noise(splits[13], (D,), 0.3, 1.5),
        "embedding": noise(splits[14], (PREFIX, D), 1.0, 6.0),
        "first_weight": noise(splits[15], (D, RHID), D ** -0.5, 0.1875),
        "first_bias": noise(splits[16], (RHID,), 0.3, 1.5),
        "second_weight": noise(splits[17], (RHID, KV_COLS), RHID ** -0.5, 0.25, ((1, 4),)),
        "second_bias": noise(splits[18], (KV_COLS,), 0.3, 1.5, ((0, 4),)),
    }


EPSILON = 1e-05
MASKED = -1000000000.0

@jax.custom_vjp
def low(v):
    return lax.optimization_barrier(v.astype(jnp.bfloat16)).astype(jnp.float32)

@jax.custom_vjp
def low_back(v):
    return v

def low_keep(v):
    return (low(v), None)

def low_pass(kept, grad):
    return (grad,)

def back_keep(v):
    return (v, None)

def back_low(kept, grad):
    return (low(grad),)
low.defvjp(low_keep, low_pass)
low_back.defvjp(back_keep, back_low)

def matmul(left, right):
    return jnp.dot(left, right, precision=lax.Precision.HIGHEST)

def norm_apply(values, gain, shift):
    average = lax.optimization_barrier(jnp.mean(values, axis=-1, keepdims=True))
    centred = values - average
    variance = lax.optimization_barrier(jnp.mean(centred * centred, axis=-1, keepdims=True))
    return centred * lax.rsqrt(variance + EPSILON) * gain + shift

def reparam(embed, first_weight, first_bias, second_weight, second_bias):
    pre_hidden = low_back(matmul(embed, first_weight) + first_bias)
    hidden = low(jnp.tanh(pre_hidden))
    return low_back(low(matmul(hidden, second_weight) + second_bias))

def block_forward(group, prefix_keys, prefix_values, trunk):
    ln1_gain, ln1_shift, qkv_weight, qkv_bias, out_weight, out_bias, ln2_gain, ln2_shift, fc_weight, fc_bias, proj_weight, proj_bias = trunk
    seq_count, length, model_width = group.shape
    head_count = prefix_keys.shape[1]
    head_size = prefix_keys.shape[2]
    flat = group.reshape(seq_count * length, model_width)
    normed = low(norm_apply(flat, ln1_gain, ln1_shift))
    packed = low_back(low(matmul(normed, qkv_weight) + qkv_bias))
    queries = packed[:, :model_width].reshape(seq_count, length, head_count, head_size)
    keys = packed[:, model_width:2 * model_width].reshape(seq_count, length, head_count, head_size)
    values = packed[:, 2 * model_width:].reshape(seq_count, length, head_count, head_size)
    scores = jnp.einsum('slhe,smhe->shlm', queries, keys, precision=lax.Precision.HIGHEST) * 0.125
    causal = lax.broadcasted_iota(jnp.int32, (length, length), 0) >= lax.broadcasted_iota(jnp.int32, (length, length), 1)
    scores = low_back(jnp.where(causal, scores, MASKED))
    prefix_scores = low_back(jnp.einsum('slhe,phe->shlp', queries, prefix_keys, precision=lax.Precision.HIGHEST) * 0.125)
    top = jnp.maximum(lax.optimization_barrier(jnp.max(scores, axis=-1, keepdims=True)), lax.optimization_barrier(jnp.max(prefix_scores, axis=-1, keepdims=True)))
    weights = jnp.exp(scores - top)
    prefix_weights = jnp.exp(prefix_scores - top)
    total = lax.optimization_barrier(jnp.sum(weights, axis=-1, keepdims=True)) + lax.optimization_barrier(jnp.sum(prefix_weights, axis=-1, keepdims=True))
    probs = low(weights / total)
    prefix_probs = low(prefix_weights / total)
    mixed = jnp.einsum('shlm,smhe->slhe', probs, values, precision=lax.Precision.HIGHEST)
    mixed = mixed + jnp.einsum('shlp,phe->slhe', prefix_probs, prefix_values, precision=lax.Precision.HIGHEST)
    attended = low_back(low(mixed.reshape(seq_count * length, model_width)))
    branch = low_back(matmul(attended, out_weight) + out_bias)
    middle = flat + branch
    normed_two = low(norm_apply(middle, ln2_gain, ln2_shift))
    pre_act = low_back(matmul(normed_two, fc_weight) + fc_bias)
    activated = low(jax.nn.gelu(pre_act, approximate=True))
    result = middle + matmul(activated, proj_weight) + proj_bias
    return result.reshape(group.shape)

def reference(tokens, cotangent, ln1_gain, ln1_shift, qkv_weight, qkv_bias, out_weight, out_bias, ln2_gain, ln2_shift, fc_weight, fc_bias, proj_weight, proj_bias, embedding, first_weight, first_bias, second_weight, second_bias):
    trunk = tuple((item.astype(jnp.float32) for item in (ln1_gain, ln1_shift, qkv_weight, qkv_bias, out_weight, out_bias, ln2_gain, ln2_shift, fc_weight, fc_bias, proj_weight, proj_bias)))
    group_size = math.gcd(SEQS, 16)
    group_count = SEQS // group_size
    model_width = tokens.shape[1]

    def forward(tokens_f, embed, weight_one, bias_one, weight_two, bias_two):
        prefix_kv = reparam(embed, weight_one, bias_one, weight_two, bias_two)
        prefix_keys = prefix_kv[:, :model_width].reshape(PREFIX, HEADS, model_width // HEADS)
        prefix_values = prefix_kv[:, model_width:].reshape(PREFIX, HEADS, model_width // HEADS)
        groups = tokens_f.reshape(group_count, group_size, SEQ_LEN, model_width)
        checked = jax.checkpoint(block_forward)

        def step(carry, group):
            return (carry, checked(group, prefix_keys, prefix_values, trunk))
        _, outputs = lax.scan(step, jnp.zeros((), jnp.float32), groups)
        return outputs.reshape(tokens_f.shape)
    result, pullback = jax.vjp(forward, tokens.astype(jnp.float32), embedding.astype(jnp.float32), first_weight.astype(jnp.float32), first_bias.astype(jnp.float32), second_weight.astype(jnp.float32), second_bias.astype(jnp.float32))
    grads = pullback(cotangent.astype(jnp.float32))
    return (result.astype(jnp.bfloat16), grads[0].astype(jnp.bfloat16), grads[1], grads[2], grads[3], grads[4], grads[5])
```

```python
import functools

import jax
import jax.numpy as jnp
from jax import lax
from jax.experimental import pallas as pl
from jax.experimental.pallas import tpu as pltpu
from jax.sharding import PartitionSpec as P

HEADS = 16
PREFIX = 10
PAD = 16
SEQ_LEN = 256
HALF = SEQ_LEN // 2
PAIR = 128
BLOCK = 256
FF_CHUNK = 512
FF_ROWS = 1024
GROUP = 2

EPSILON = 1e-05
MASKED = -1000000000.0
NEVER = -1e30
ROOT = 0.7978845608028654
CUBIC = 0.044715

F32 = jnp.float32
BF16 = jnp.bfloat16
NN = (((1,), (0,)), ((), ()))
NT = (((1,), (1,)), ((), ()))
TN = (((0,), (0,)), ((), ()))
MESH = pl.DeviceIdType.MESH


def dot(left, right, form=NN):
    return lax.dot_general(left, right, form, preferred_element_type=F32)


def row(ref):
    return ref[...].astype(F32).reshape(1, -1)


def normalise(values):
    average = jnp.mean(values, axis=-1, keepdims=True)
    centred = values - average
    variance = jnp.mean(centred * centred, axis=-1, keepdims=True)
    scale = lax.rsqrt(variance + EPSILON)
    return centred * scale, scale


def norm_pull(values, gain, upstream):
    unit, scale = normalise(values)
    scaled = upstream * gain
    first = jnp.mean(scaled, axis=-1, keepdims=True)
    second = jnp.mean(scaled * unit, axis=-1, keepdims=True)
    return scale * (scaled - first - unit * second)


def gelu_and_slope(values):
    square = values * values
    inner = jnp.tanh(values * (ROOT + (ROOT * CUBIC) * square))
    half = 0.5 * inner + 0.5
    bend = (0.5 - 0.5 * inner * inner) * (ROOT + (3.0 * ROOT * CUBIC) * square)
    return values * half, half + values * bend


def head_lanes():
    lane = lax.broadcasted_iota(jnp.int32, (1, PAIR), 1)
    return (lane < PAIR // 2, lane >= PAIR // 2)


def columns(base, pair):
    return pl.ds(base + pair * PAIR, PAIR)


def over_rows(row_count, group, body):
    def step(index, carry):
        for place in range(group):
            block = index * group + place
            body(block, pl.ds(pl.multiple_of(block * BLOCK, BLOCK), BLOCK))
        return carry

    lax.fori_loop(0, row_count // (BLOCK * group), step, 0)


def attention_forward(seq, width, packed, prefix, attended, top, bottom, side):
    rows = pl.ds(pl.multiple_of(seq * SEQ_LEN, SEQ_LEN), SEQ_LEN)
    pairs = width // PAIR
    key = lax.broadcasted_iota(jnp.int32, (HALF, HALF), 0)
    query = lax.broadcasted_iota(jnp.int32, (HALF, HALF), 1)
    causal = key <= query
    real = lax.broadcasted_iota(jnp.int32, (PAD, 1), 0) < PREFIX
    lanes = head_lanes()
    scores = []
    for pair in range(pairs):
        queries = packed[rows, columns(0, pair)]
        keys = packed[rows, columns(width, pair)]
        prefix_keys = prefix[:, columns(0, pair)]
        for mine in lanes:
            scores.append(
                (
                    dot(jnp.where(mine, keys, 0), queries, NT),
                    dot(jnp.where(mine, prefix_keys, 0), queries, NT),
                )
            )
    probs = []
    for full, extra in scores:
        extra = jnp.where(real, extra, NEVER)
        early = jnp.where(causal, full[:HALF, :HALF], MASKED)
        cross = full[:HALF, HALF:]
        late = jnp.where(causal, full[HALF:, HALF:], MASKED)
        peak = jnp.max(extra, axis=0, keepdims=True)
        peak_early = jnp.maximum(jnp.max(early, axis=0, keepdims=True), peak[:, :HALF])
        peak_late = jnp.maximum(
            jnp.maximum(
                jnp.max(cross, axis=0, keepdims=True), jnp.max(late, axis=0, keepdims=True)
            ),
            peak[:, HALF:],
        )
        early = jnp.exp(early - peak_early)
        cross = jnp.exp(cross - peak_late)
        late = jnp.exp(late - peak_late)
        extra = jnp.exp(extra - jnp.concatenate([peak_early, peak_late], axis=1))
        total = jnp.sum(extra, axis=0, keepdims=True)
        total_early = jnp.sum(early, axis=0, keepdims=True) + total[:, :HALF]
        total_late = (
            jnp.sum(cross, axis=0, keepdims=True)
            + jnp.sum(late, axis=0, keepdims=True)
            + total[:, HALF:]
        )
        inverse = 1.0 / jnp.concatenate([total_early, total_late], axis=1)
        first = jnp.concatenate(
            [
                (early * inverse[:, :HALF]).astype(BF16),
                (cross * inverse[:, HALF:]).astype(BF16),
            ],
            axis=1,
        )
        probs.append(
            (first, (late * inverse[:, HALF:]).astype(BF16), (extra * inverse).astype(BF16))
        )
    empty = jnp.zeros((HALF, HALF), BF16)
    for pair in range(pairs):
        values = packed[rows, columns(2 * width, pair)].T
        prefix_values = prefix[:, columns(width, pair)].T
        halves = []
        for head in (0, 1):
            first, second, extra = probs[2 * pair + head]
            place = seq * HEADS + 2 * pair + head
            top[place] = first
            bottom[place] = second
            side[place] = extra
            whole = jnp.concatenate([first, jnp.concatenate([empty, second], axis=1)], axis=0)
            mine = slice(head * (PAIR // 2), (head + 1) * (PAIR // 2))
            halves.append(dot(values[mine], whole) + dot(prefix_values[mine], extra))
        attended[rows, columns(0, pair)] = jnp.concatenate(halves, axis=0).astype(BF16).T


def attention_backward(
    seq, width, packed, prefix, upstream, attended, top, bottom, side, prefix_grad
):
    rows = pl.ds(pl.multiple_of(seq * SEQ_LEN, SEQ_LEN), SEQ_LEN)
    pairs = width // PAIR
    lanes = head_lanes()
    head_row = lax.broadcasted_iota(jnp.int32, (8, PAIR), 0)
    head_lane = lax.broadcasted_iota(jnp.int32, (8, PAIR), 1)
    picker = jnp.where(head_lane // (PAIR // 2) == head_row, 1.0, 0.0).astype(BF16)
    empty = jnp.zeros((HALF, HALF), BF16)
    incoming, deltas = [], []
    for pair in range(pairs):
        grad = upstream[rows, columns(0, pair)]
        deltas.append(dot(picker, grad * attended[rows, columns(0, pair)], NT))
        values = packed[rows, columns(2 * width, pair)]
        prefix_values = prefix[:, columns(width, pair)]
        for mine in lanes:
            incoming.append(
                (
                    dot(jnp.where(mine, values, 0), grad, NT),
                    dot(jnp.where(mine, prefix_values, 0), grad, NT),
                )
            )
    slopes = []
    for pair in range(pairs):
        for head in (0, 1):
            place = seq * HEADS + 2 * pair + head
            full, extra = incoming[2 * pair + head]
            delta = deltas[pair][head : head + 1, :]
            first = (top[place].astype(F32) * (full[:HALF] - delta)).astype(BF16)
            second = (bottom[place].astype(F32) * (full[HALF:, HALF:] - delta[:, HALF:])).astype(
                BF16
            )
            extra = (side[place].astype(F32) * (extra - delta)).astype(BF16)
            slopes.append((first, second, extra))
    for pair in range(pairs):
        grad = upstream[rows, columns(0, pair)]
        queries = packed[rows, columns(0, pair)]
        keys = packed[rows, columns(width, pair)].T
        prefix_keys = prefix[:, columns(0, pair)].T
        place = seq * HEADS + 2 * pair

        def pulled(stream, first, second, extra):
            masked = [jnp.where(mine, stream, 0) for mine in lanes]
            both = jnp.concatenate(masked, axis=0)
            late = jnp.concatenate([part[HALF:] for part in masked], axis=0)
            joined = [jnp.concatenate(part, axis=1) for part in (first, second, extra)]
            return dot(joined[0], both), dot(joined[1], late), dot(joined[2], both)

        left, right = slopes[2 * pair], slopes[2 * pair + 1]
        key_first, key_second, key_extra = pulled(
            queries, (left[0], right[0]), (left[1], right[1]), (left[2], right[2])
        )
        value_first, value_second, value_extra = pulled(
            grad,
            (top[place], top[place + 1]),
            (bottom[place], bottom[place + 1]),
            (side[place], side[place + 1]),
        )
        halves = []
        for head in (0, 1):
            first, second, extra = slopes[2 * pair + head]
            whole = jnp.concatenate([first, jnp.concatenate([empty, second], axis=1)], axis=0)
            mine = slice(head * (PAIR // 2), (head + 1) * (PAIR // 2))
            halves.append(dot(keys[mine], whole) + dot(prefix_keys[mine], extra))
        prefix_grad[:, columns(0, pair)] += key_extra
        prefix_grad[:, columns(width, pair)] += value_extra
        packed[rows, columns(0, pair)] = (
            (jnp.concatenate(halves, axis=0) * 0.125).astype(BF16).T
        )
        packed[rows, columns(width, pair)] = jnp.concatenate(
            [key_first, key_second], axis=0
        ).astype(BF16)
        packed[rows, columns(2 * width, pair)] = jnp.concatenate(
            [value_first, value_second], axis=0
        ).astype(BF16)


def layer_kernel(
    dp_size,
    col_size,
    tokens_hbm,
    cotangent_hbm,
    qkv_hbm,
    out_hbm,
    fc_hbm,
    proj_hbm,
    first_hbm,
    second_hbm,
    ln1_gain,
    ln1_shift,
    qkv_bias,
    out_bias,
    ln2_gain,
    ln2_shift,
    fc_bias,
    proj_bias,
    embedding,
    first_bias,
    second_bias,
    block_hbm,
    grad_hbm,
    hidden_out,
    owned_out,
    pre_out,
    stream,
    wide,
    out_weight,
    fc_weight,
    proj_weight,
    packed,
    top,
    bottom,
    side,
    attended,
    middle,
    normed,
    activated,
    second_weight,
    prefix,
    prefix_grad,
    padded,
    parts_col,
    parts_dp,
    parts_hidden,
    load_sem,
    store_sem,
    gather_send,
    gather_recv,
    scatter_send,
    scatter_recv,
    reduce_send,
    reduce_recv,
    hidden_send,
    hidden_recv,
):
    row_count, width = stream.shape
    ff = activated.shape[1]
    tokens = wide.at[pl.ds(0, row_count), pl.ds(3 * width, width)]
    hidden_width = second_weight.shape[0]
    owned = second_weight.shape[1]
    seqs = row_count // SEQ_LEN
    my_dp = lax.axis_index("dp")
    my_col = lax.axis_index("col")

    def col_peer(step):
        return (my_dp, lax.rem(my_col + step, col_size))

    def dp_peer(step):
        return (lax.rem(my_dp + step, dp_size), my_col)

    barrier = pltpu.get_barrier_semaphore()
    for step in range(1, col_size):
        pl.semaphore_signal(barrier, inc=1, device_id=col_peer(step), device_id_type=MESH)
    for step in range(1, dp_size):
        pl.semaphore_signal(barrier, inc=1, device_id=dp_peer(step), device_id_type=MESH)

    first_weight = activated.at[pl.ds(0, width), pl.ds(0, hidden_width)]
    thirds = [pl.ds(third * width, width) for third in range(3)]
    qkv_weight = [wide.at[pl.ds(0, width), third] for third in thirds]
    loads = [
        pltpu.make_async_copy(source, target, load_sem.at[place])
        for place, (source, target) in enumerate(
            [
                (first_hbm, first_weight),
                (second_hbm, second_weight),
                (tokens_hbm, tokens),
                (qkv_hbm.at[:, thirds[0]], qkv_weight[0]),
                (qkv_hbm.at[:, thirds[1]], qkv_weight[1]),
                (qkv_hbm.at[:, thirds[2]], qkv_weight[2]),
                (out_hbm, out_weight),
                (fc_hbm, fc_weight),
                (proj_hbm, proj_weight),
                (cotangent_hbm, stream),
            ]
        )
    ]
    for load in loads:
        load.start()

    padded[...] = jnp.zeros_like(padded)
    padded[0:PREFIX, :] = embedding[...].astype(F32)
    loads[0].wait()
    loads[1].wait()
    pre_hidden = dot(padded[...].astype(BF16), first_weight[...]) + row(first_bias)
    hidden_full = jnp.tanh(pre_hidden)
    hidden_low = hidden_full.astype(BF16)
    hidden_out[...] = hidden_low
    owned_kv = dot(hidden_low, second_weight[...]) + row(second_bias)
    mine = pl.ds(pl.multiple_of(my_col * owned, PAIR), owned)
    prefix[:, mine] = owned_kv.astype(BF16)
    pl.semaphore_wait(barrier, col_size + dp_size - 2)
    gathers = [
        pltpu.make_async_remote_copy(
            src_ref=prefix.at[:, mine],
            dst_ref=prefix.at[:, mine],
            send_sem=gather_send.at[step - 1],
            recv_sem=gather_recv.at[step - 1],
            device_id=col_peer(step),
            device_id_type=MESH,
        )
        for step in range(1, col_size)
    ]
    for gather in gathers:
        gather.start()

    loads[2].wait()
    gain_one, shift_one = row(ln1_gain), row(ln1_shift)

    def first_norm(block, rows):
        unit, _ = normalise(tokens[rows, :].astype(F32))
        normed[rows, :] = (unit * gain_one + shift_one).astype(BF16)

    over_rows(row_count, GROUP, first_norm)
    for third in range(3):
        loads[3 + third].wait()
        bias = qkv_bias[pl.ds(third * width, width)].astype(F32).reshape(1, -1)
        part = (dot(normed[...], qkv_weight[third][...]) + bias).astype(BF16)
        packed[:, thirds[third]] = part * BF16(0.125) if third == 0 else part

    for gather in gathers:
        gather.wait()

    def forward_step(seq, carry):
        attention_forward(seq, width, packed, prefix, attended, top, bottom, side)
        return carry

    lax.fori_loop(0, seqs, forward_step, 0)

    loads[6].wait()
    bias = row(out_bias)
    gain_two, shift_two = row(ln2_gain), row(ln2_shift)

    def output_rows(block, rows):
        total = tokens[rows, :].astype(F32) + dot(attended[rows, :], out_weight[...]) + bias
        middle[rows, :] = total
        unit, _ = normalise(total)
        normed[rows, :] = (unit * gain_two + shift_two).astype(BF16)

    over_rows(row_count, GROUP, output_rows)

    loads[7].wait()
    loads[8].wait()
    loads[9].wait()

    def ff_step(chunk, carry):
        units = pl.ds(pl.multiple_of(chunk * FF_CHUNK, FF_CHUNK), FF_CHUNK)
        bias = fc_bias[:, units]
        for start in range(0, row_count, FF_ROWS):
            rows = pl.ds(start, FF_ROWS)
            pre_act = dot(normed[rows, :], fc_weight[:, units]) + bias
            upstream = dot(stream[rows, :], proj_weight[units, :], NT)
            value, slope = gelu_and_slope(pre_act)
            activated[rows, units] = value.astype(BF16)
            wide[rows, units] = (slope * upstream).astype(BF16)
        return carry

    lax.fori_loop(0, ff // FF_CHUNK, ff_step, 0)

    def middle_rows(block, rows):
        upstream = dot(wide[rows, :], fc_weight[...], NT)
        total = stream[rows, :].astype(F32) + norm_pull(middle[rows, :], gain_two, upstream)
        low = total.astype(BF16)
        stream[rows, :] = low
        normed[rows, :] = dot(low, out_weight[...], NT).astype(BF16)

    over_rows(row_count, GROUP, middle_rows)

    reloads = [
        pltpu.make_async_copy(source, target, load_sem.at[2 + place])
        for place, (source, target) in enumerate(
            [(tokens_hbm, tokens)]
            + [(qkv_hbm.at[:, thirds[third]], qkv_weight[third]) for third in range(3)]
        )
    ]
    for load in reloads:
        load.start()

    prefix_grad[...] = jnp.zeros_like(prefix_grad)

    def backward_step(seq, carry):
        attention_backward(
            seq, width, packed, prefix, normed, attended, top, bottom, side, prefix_grad
        )
        return carry

    lax.fori_loop(0, seqs, backward_step, 0)

    scatters = [
        pltpu.make_async_remote_copy(
            src_ref=prefix_grad.at[
                :, pl.ds(pl.multiple_of(lax.rem(my_col + step, col_size) * owned, PAIR), owned)
            ],
            dst_ref=parts_col.at[step - 1],
            send_sem=scatter_send.at[step - 1],
            recv_sem=scatter_recv.at[step - 1],
            device_id=col_peer(step),
            device_id_type=MESH,
        )
        for step in range(1, col_size)
    ]
    reduces = [
        pltpu.make_async_remote_copy(
            src_ref=parts_dp.at[my_dp],
            dst_ref=parts_dp.at[my_dp],
            send_sem=reduce_send.at[step - 1],
            recv_sem=reduce_recv.at[step - 1],
            device_id=dp_peer(step),
            device_id_type=MESH,
        )
        for step in range(1, dp_size)
    ]
    hiddens = [
        pltpu.make_async_remote_copy(
            src_ref=parts_hidden.at[my_col],
            dst_ref=parts_hidden.at[my_col],
            send_sem=hidden_send.at[step - 1],
            recv_sem=hidden_recv.at[step - 1],
            device_id=col_peer(step),
            device_id_type=MESH,
        )
        for step in range(1, col_size)
    ]

    def exchange(stage):
        if stage == 0:
            for scatter in scatters:
                scatter.start()
        elif stage == 1:
            for scatter in scatters:
                scatter.wait()
            total = prefix_grad[:, mine]
            for step in range(1, col_size):
                total = total + parts_col[step - 1]
            parts_dp[my_dp] = total
            for reduce in reduces:
                reduce.start()
        elif stage == 2:
            for reduce in reduces:
                reduce.wait()
            total = parts_dp[0]
            for step in range(1, dp_size):
                total = total + parts_dp[step]
            low = total.astype(BF16)
            owned_out[...] = low
            parts_hidden[my_col] = dot(low, second_weight[...], NT)
            for part in hiddens:
                part.start()
        else:
            for part in hiddens:
                part.wait()
            total = parts_hidden[0]
            for step in range(1, col_size):
                total = total + parts_hidden[step]
            first_weight_sum = hidden_full * hidden_full
            pre_out[...] = (total * (1.0 - first_weight_sum)).astype(BF16)

    def store(source, target, place, rows):
        return pltpu.make_async_copy(
            source.at[rows, :], target.at[rows, :], store_sem.at[place]
        )

    blocks = row_count // BLOCK
    proj_row = row(proj_bias)
    exchange(0)

    def block_rows(block, rows):
        total = middle[rows, :] + dot(activated[rows, :], proj_weight[...]) + proj_row
        attended[rows, :] = total.astype(BF16)
        store(attended, block_hbm, block, rows).start()
        pl.when(block == 0)(lambda: exchange(1))
        pl.when(block == blocks - 2)(lambda: exchange(2))

    over_rows(row_count, 1, block_rows)
    for load in reloads:
        load.wait()

    def grad_rows(block, rows):
        upstream = dot(packed[rows, :], wide[0:width, 0 : 3 * width], NT)
        total = stream[rows, :].astype(F32) + norm_pull(
            tokens[rows, :].astype(F32), gain_one, upstream
        )
        tokens[rows, :] = total.astype(BF16)
        store(tokens, grad_hbm, blocks + block, rows).start()

    over_rows(row_count, GROUP, grad_rows)
    exchange(3)
    for block in range(blocks):
        rows = pl.ds(block * BLOCK, BLOCK)
        store(attended, block_hbm, block, rows).wait()
        store(tokens, grad_hbm, blocks + block, rows).wait()


def small_kernel(
    embedding, first_weight, hidden, owned, pre, embed_grad, first_grad, first_bias_grad,
    second_grad, second_bias_grad, padded
):
    padded[...] = jnp.zeros_like(padded)
    padded[0:PREFIX, :] = embedding[...].astype(F32)
    low = padded[...].astype(BF16)
    first_grad[...] = dot(low, pre[...], TN)
    second_grad[...] = dot(hidden[...], owned[...], TN)
    embed_grad[...] = dot(pre[...], first_weight[...], NT)[:PREFIX]
    first_bias_grad[...] = jnp.sum(pre[...].astype(F32), axis=0)
    second_bias_grad[...] = jnp.sum(owned[...].astype(F32), axis=0)


def shards(
    dp_size,
    col_size,
    tokens,
    cotangent,
    ln1_gain,
    ln1_shift,
    qkv_weight,
    qkv_bias,
    out_weight,
    out_bias,
    ln2_gain,
    ln2_shift,
    fc_weight,
    fc_bias,
    proj_weight,
    proj_bias,
    embedding,
    first_weight,
    first_bias,
    second_weight,
    second_bias,
):
    row_count, width = tokens.shape
    ff = fc_weight.shape[1]
    hidden_width, owned = second_weight.shape
    heads = row_count // SEQ_LEN * HEADS
    anywhere = pl.BlockSpec(memory_space=pl.ANY)
    local = pl.BlockSpec(memory_space=pltpu.VMEM)
    dma = pltpu.SemaphoreType.DMA
    block_out, token_grad, hidden, owned_grad, pre_grad = pl.pallas_call(
        functools.partial(layer_kernel, dp_size, col_size),
        out_shape=(
            jax.ShapeDtypeStruct((row_count, width), BF16),
            jax.ShapeDtypeStruct((row_count, width), BF16),
            jax.ShapeDtypeStruct((PAD, hidden_width), BF16),
            jax.ShapeDtypeStruct((PAD, owned), BF16),
            jax.ShapeDtypeStruct((PAD, hidden_width), BF16),
        ),
        in_specs=[anywhere] * 8 + [local] * 11,
        out_specs=[anywhere] * 2 + [local] * 3,
        scratch_shapes=[
            pltpu.VMEM((row_count, width), BF16),
            pltpu.VMEM((max(row_count, width), ff), BF16),
            pltpu.VMEM((width, width), BF16),
            pltpu.VMEM((width, ff), BF16),
            pltpu.VMEM((ff, width), BF16),
            pltpu.VMEM((row_count, 3 * width), BF16),
            pltpu.VMEM((heads, HALF, SEQ_LEN), BF16),
            pltpu.VMEM((heads, HALF, HALF), BF16),
            pltpu.VMEM((heads, PAD, SEQ_LEN), BF16),
            pltpu.VMEM((row_count, width), BF16),
            pltpu.VMEM((row_count, width), F32),
            pltpu.VMEM((row_count, width), BF16),
            pltpu.VMEM((max(row_count, width), ff), BF16),
            pltpu.VMEM((hidden_width, owned), BF16),
            pltpu.VMEM((PAD, col_size * owned), BF16),
            pltpu.VMEM((PAD, col_size * owned), F32),
            pltpu.VMEM((PAD, width), F32),
            pltpu.VMEM((col_size - 1, PAD, owned), F32),
            pltpu.VMEM((dp_size, PAD, owned), F32),
            pltpu.VMEM((col_size, PAD, hidden_width), F32),
            dma((10,)),
            dma((2 * (row_count // BLOCK),)),
            dma((col_size - 1,)),
            dma((col_size - 1,)),
            dma((col_size - 1,)),
            dma((col_size - 1,)),
            dma((dp_size - 1,)),
            dma((dp_size - 1,)),
            dma((col_size - 1,)),
            dma((col_size - 1,)),
        ],
        compiler_params=pltpu.CompilerParams(
            collective_id=0, has_side_effects=True, vmem_limit_bytes=63 * 2**20
        ),
        name="layer",
    )(
        tokens,
        cotangent,
        qkv_weight,
        out_weight,
        fc_weight,
        proj_weight,
        first_weight,
        second_weight,
        ln1_gain,
        ln1_shift,
        qkv_bias,
        out_bias,
        ln2_gain,
        ln2_shift,
        fc_bias.astype(F32).reshape(1, -1),
        proj_bias,
        embedding,
        first_bias,
        second_bias,
    )
    embed_grad, first_grad, first_bias_grad, second_grad, second_bias_grad = pl.pallas_call(
        small_kernel,
        out_shape=(
            jax.ShapeDtypeStruct((PREFIX, width), F32),
            jax.ShapeDtypeStruct((width, hidden_width), F32),
            jax.ShapeDtypeStruct((hidden_width,), F32),
            jax.ShapeDtypeStruct((hidden_width, owned), F32),
            jax.ShapeDtypeStruct((owned,), F32),
        ),
        in_specs=[local] * 5,
        out_specs=[local] * 5,
        scratch_shapes=[pltpu.VMEM((PAD, width), F32)],
        name="small_grads",
    )(embedding, first_weight, hidden, owned_grad, pre_grad)
    return (
        block_out,
        token_grad,
        embed_grad,
        first_grad,
        first_bias_grad,
        second_grad,
        second_bias_grad,
    )


def solution(mesh):
    placed = (
        P(("dp", "col"), None),
        P(("dp", "col"), None),
        P(),
        P(),
        P(),
        P(),
        P(),
        P(),
        P(),
        P(),
        P(),
        P(),
        P(),
        P(),
        P(),
        P(),
        P(),
        P(None, "col"),
        P("col"),
    )
    return jax.shard_map(
        functools.partial(shards, mesh.shape["dp"], mesh.shape["col"]),
        mesh=mesh,
        in_specs=placed,
        out_specs=(
            P(("dp", "col"), None),
            P(("dp", "col"), None),
            P(),
            P(),
            P(),
            P(None, "col"),
            P("col"),
        ),
        check_vma=False,
    )
```

```python
import functools

import jax
import jax.numpy as jnp
from jax import lax
from jax.experimental import pallas as pl
from jax.experimental.pallas import tpu as pltpu
from jax.sharding import PartitionSpec as P

HEADS = 16
PREFIX = 10
PAD = 16
SEQ_LEN = 256
HALF = SEQ_LEN // 2
PAIR = 128
BLOCK = 256
FF_CHUNK = 512
FF_ROWS = 1024
GROUP = 2

EPSILON = 1e-05
MASKED = -1000000000.0
NEVER = -1e30
ROOT = 0.7978845608028654
CUBIC = 0.044715

F32 = jnp.float32
BF16 = jnp.bfloat16
NN = (((1,), (0,)), ((), ()))
NT = (((1,), (1,)), ((), ()))
TN = (((0,), (0,)), ((), ()))
MESH = pl.DeviceIdType.MESH


def dot(left, right, form=NN):
    return lax.dot_general(left, right, form, preferred_element_type=F32)


def row(ref):
    return ref[...].astype(F32).reshape(1, -1)


def normalise(values):
    average = jnp.mean(values, axis=-1, keepdims=True)
    centred = values - average
    variance = jnp.mean(centred * centred, axis=-1, keepdims=True)
    scale = lax.rsqrt(variance + EPSILON)
    return centred * scale, scale


def norm_pull(values, gain, upstream):
    unit, scale = normalise(values)
    scaled = upstream * gain
    first = jnp.mean(scaled, axis=-1, keepdims=True)
    second = jnp.mean(scaled * unit, axis=-1, keepdims=True)
    return scale * (scaled - first - unit * second)


def gelu_and_slope(values):
    square = values * values
    inner = jnp.tanh(values * (ROOT + (ROOT * CUBIC) * square))
    half = 0.5 * inner + 0.5
    bend = (0.5 - 0.5 * inner * inner) * (ROOT + (3.0 * ROOT * CUBIC) * square)
    return values * half, half + values * bend


def head_lanes():
    lane = lax.broadcasted_iota(jnp.int32, (1, PAIR), 1)
    return (lane < PAIR // 2, lane >= PAIR // 2)


def columns(base, pair):
    return pl.ds(base + pair * PAIR, PAIR)


def over_rows(row_count, group, body):
    def step(index, carry):
        for place in range(group):
            block = index * group + place
            body(block, pl.ds(pl.multiple_of(block * BLOCK, BLOCK), BLOCK))
        return carry

    lax.fori_loop(0, row_count // (BLOCK * group), step, 0)


def attention_forward(seq, width, packed, prefix, attended, top, bottom, side):
    rows = pl.ds(pl.multiple_of(seq * SEQ_LEN, SEQ_LEN), SEQ_LEN)
    pairs = width // PAIR
    key = lax.broadcasted_iota(jnp.int32, (HALF, HALF), 0)
    query = lax.broadcasted_iota(jnp.int32, (HALF, HALF), 1)
    causal = key <= query
    real = lax.broadcasted_iota(jnp.int32, (PAD, 1), 0) < PREFIX
    lanes = head_lanes()
    scores = []
    for pair in range(pairs):
        queries = packed[rows, columns(0, pair)]
        keys = packed[rows, columns(width, pair)]
        prefix_keys = prefix[:, columns(0, pair)]
        for mine in lanes:
            scores.append(
                (
                    dot(jnp.where(mine, keys, 0), queries, NT),
                    dot(jnp.where(mine, prefix_keys, 0), queries, NT),
                )
            )
    probs = []
    for full, extra in scores:
        extra = jnp.where(real, extra, NEVER)
        early = jnp.where(causal, full[:HALF, :HALF], MASKED)
        cross = full[:HALF, HALF:]
        late = jnp.where(causal, full[HALF:, HALF:], MASKED)
        peak = jnp.max(extra, axis=0, keepdims=True)
        peak_early = jnp.maximum(jnp.max(early, axis=0, keepdims=True), peak[:, :HALF])
        peak_late = jnp.maximum(
            jnp.maximum(
                jnp.max(cross, axis=0, keepdims=True), jnp.max(late, axis=0, keepdims=True)
            ),
            peak[:, HALF:],
        )
        early = jnp.exp(early - peak_early)
        cross = jnp.exp(cross - peak_late)
        late = jnp.exp(late - peak_late)
        extra = jnp.exp(extra - jnp.concatenate([peak_early, peak_late], axis=1))
        total = jnp.sum(extra, axis=0, keepdims=True)
        total_early = jnp.sum(early, axis=0, keepdims=True) + total[:, :HALF]
        total_late = (
            jnp.sum(cross, axis=0, keepdims=True)
            + jnp.sum(late, axis=0, keepdims=True)
            + total[:, HALF:]
        )
        inverse = 1.0 / jnp.concatenate([total_early, total_late], axis=1)
        first = jnp.concatenate(
            [
                (early * inverse[:, :HALF]).astype(BF16),
                (cross * inverse[:, HALF:]).astype(BF16),
            ],
            axis=1,
        )
        probs.append(
            (first, (late * inverse[:, HALF:]).astype(BF16), (extra * inverse).astype(BF16))
        )
    empty = jnp.zeros((HALF, HALF), BF16)
    for pair in range(pairs):
        values = packed[rows, columns(2 * width, pair)].T
        prefix_values = prefix[:, columns(width, pair)].T
        halves = []
        for head in (0, 1):
            first, second, extra = probs[2 * pair + head]
            place = seq * HEADS + 2 * pair + head
            top[place] = first
            bottom[place] = second
            side[place] = extra
            whole = jnp.concatenate([first, jnp.concatenate([empty, second], axis=1)], axis=0)
            mine = slice(head * (PAIR // 2), (head + 1) * (PAIR // 2))
            halves.append(dot(values[mine], whole) + dot(prefix_values[mine], extra))
        attended[rows, columns(0, pair)] = jnp.concatenate(halves, axis=0).astype(BF16).T


def attention_backward(
    seq, width, packed, prefix, upstream, attended, top, bottom, side, prefix_grad
):
    rows = pl.ds(pl.multiple_of(seq * SEQ_LEN, SEQ_LEN), SEQ_LEN)
    pairs = width // PAIR
    lanes = head_lanes()
    head_row = lax.broadcasted_iota(jnp.int32, (8, PAIR), 0)
    head_lane = lax.broadcasted_iota(jnp.int32, (8, PAIR), 1)
    picker = jnp.where(head_lane // (PAIR // 2) == head_row, 1.0, 0.0).astype(BF16)
    empty = jnp.zeros((HALF, HALF), BF16)
    incoming, deltas = [], []
    for pair in range(pairs):
        grad = upstream[rows, columns(0, pair)]
        deltas.append(dot(picker, grad * attended[rows, columns(0, pair)], NT))
        values = packed[rows, columns(2 * width, pair)]
        prefix_values = prefix[:, columns(width, pair)]
        for mine in lanes:
            incoming.append(
                (
                    dot(jnp.where(mine, values, 0), grad, NT),
                    dot(jnp.where(mine, prefix_values, 0), grad, NT),
                )
            )
    slopes = []
    for pair in range(pairs):
        for head in (0, 1):
            place = seq * HEADS + 2 * pair + head
            full, extra = incoming[2 * pair + head]
            delta = deltas[pair][head : head + 1, :]
            first = (top[place].astype(F32) * (full[:HALF] - delta)).astype(BF16)
            second = (bottom[place].astype(F32) * (full[HALF:, HALF:] - delta[:, HALF:])).astype(
                BF16
            )
            extra = (side[place].astype(F32) * (extra - delta)).astype(BF16)
            slopes.append((first, second, extra))
    for pair in range(pairs):
        grad = upstream[rows, columns(0, pair)]
        queries = packed[rows, columns(0, pair)]
        keys = packed[rows, columns(width, pair)].T
        prefix_keys = prefix[:, columns(0, pair)].T
        place = seq * HEADS + 2 * pair

        def pulled(stream, first, second, extra):
            masked = [jnp.where(mine, stream, 0) for mine in lanes]
            both = jnp.concatenate(masked, axis=0)
            late = jnp.concatenate([part[HALF:] for part in masked], axis=0)
            joined = [jnp.concatenate(part, axis=1) for part in (first, second, extra)]
            return dot(joined[0], both), dot(joined[1], late), dot(joined[2], both)

        left, right = slopes[2 * pair], slopes[2 * pair + 1]
        key_first, key_second, key_extra = pulled(
            queries, (left[0], right[0]), (left[1], right[1]), (left[2], right[2])
        )
        value_first, value_second, value_extra = pulled(
            grad,
            (top[place], top[place + 1]),
            (bottom[place], bottom[place + 1]),
            (side[place], side[place + 1]),
        )
        halves = []
        for head in (0, 1):
            first, second, extra = slopes[2 * pair + head]
            whole = jnp.concatenate([first, jnp.concatenate([empty, second], axis=1)], axis=0)
            mine = slice(head * (PAIR // 2), (head + 1) * (PAIR // 2))
            halves.append(dot(keys[mine], whole) + dot(prefix_keys[mine], extra))
        prefix_grad[:, columns(0, pair)] += key_extra
        prefix_grad[:, columns(width, pair)] += value_extra
        packed[rows, columns(0, pair)] = (
            (jnp.concatenate(halves, axis=0) * 0.125).astype(BF16).T
        )
        packed[rows, columns(width, pair)] = jnp.concatenate(
            [key_first, key_second], axis=0
        ).astype(BF16)
        packed[rows, columns(2 * width, pair)] = jnp.concatenate(
            [value_first, value_second], axis=0
        ).astype(BF16)


def layer_kernel(
    dp_size,
    col_size,
    tokens_hbm,
    cotangent_hbm,
    qkv_hbm,
    out_hbm,
    fc_hbm,
    proj_hbm,
    first_hbm,
    second_hbm,
    ln1_gain,
    ln1_shift,
    qkv_bias,
    out_bias,
    ln2_gain,
    ln2_shift,
    fc_bias,
    proj_bias,
    embedding,
    first_bias,
    second_bias,
    attended,
    stream,
    hidden_out,
    owned_out,
    pre_out,
    embed_out,
    wide,
    out_weight,
    fc_weight,
    proj_weight,
    packed,
    top,
    bottom,
    side,
    middle,
    normed,
    activated,
    second_weight,
    prefix,
    prefix_grad,
    padded,
    ff_bias,
    parts_col,
    parts_dp,
    parts_hidden,
    load_sem,
    gather_send,
    gather_recv,
    scatter_send,
    scatter_recv,
    reduce_send,
    reduce_recv,
    hidden_send,
    hidden_recv,
):
    row_count, width = stream.shape
    ff = activated.shape[1]
    tokens = wide.at[pl.ds(0, row_count), pl.ds(3 * width, width)]
    hidden_width = second_weight.shape[0]
    owned = second_weight.shape[1]
    seqs = row_count // SEQ_LEN
    my_dp = lax.axis_index("dp")
    my_col = lax.axis_index("col")

    def col_peer(step):
        return (my_dp, lax.rem(my_col + step, col_size))

    def dp_peer(step):
        return (lax.rem(my_dp + step, dp_size), my_col)

    barrier = pltpu.get_barrier_semaphore()
    for step in range(1, col_size):
        pl.semaphore_signal(barrier, inc=1, device_id=col_peer(step), device_id_type=MESH)
    for step in range(1, dp_size):
        pl.semaphore_signal(barrier, inc=1, device_id=dp_peer(step), device_id_type=MESH)

    first_weight = activated.at[pl.ds(0, width), pl.ds(0, hidden_width)]
    thirds = [pl.ds(third * width, width) for third in range(3)]
    qkv_weight = [wide.at[pl.ds(0, width), third] for third in thirds]
    blocks = row_count // BLOCK
    block_rows = [pl.ds(block * BLOCK, BLOCK) for block in range(blocks)]
    loads = [
        pltpu.make_async_copy(source, target, load_sem.at[place])
        for place, (source, target) in enumerate(
            [(tokens_hbm.at[rows, :], tokens.at[rows, :]) for rows in block_rows]
            + [(first_hbm, first_weight), (second_hbm, second_weight)]
            + [(qkv_hbm.at[:, thirds[third]], qkv_weight[third]) for third in range(3)]
            + [
                (out_hbm, out_weight),
                (fc_hbm, fc_weight),
                (proj_hbm, proj_weight),
                (cotangent_hbm, stream),
            ]
        )
    ]
    for load in loads:
        load.start()
    token_loads, loads = loads[:blocks], loads[blocks:]

    padded[...] = jnp.zeros_like(padded)
    padded[0:PREFIX, :] = embedding[...].astype(F32)
    ff_bias[...] = row(fc_bias)

    gain_one, shift_one = row(ln1_gain), row(ln1_shift)
    for load, rows in zip(token_loads, block_rows):
        load.wait()
        unit, _ = normalise(tokens[rows, :].astype(F32))
        normed[rows, :] = (unit * gain_one + shift_one).astype(BF16)

    loads[0].wait()
    loads[1].wait()
    embed_out[...] = padded[...].astype(BF16)
    pre_hidden = dot(embed_out[...], first_weight[...]) + row(first_bias)
    hidden_full = jnp.tanh(pre_hidden)
    hidden_low = hidden_full.astype(BF16)
    hidden_out[...] = hidden_low
    owned_kv = dot(hidden_low, second_weight[...]) + row(second_bias)
    mine = pl.ds(pl.multiple_of(my_col * owned, PAIR), owned)
    prefix[:, mine] = owned_kv.astype(BF16)
    gathers = [
        pltpu.make_async_remote_copy(
            src_ref=prefix.at[:, mine],
            dst_ref=prefix.at[:, mine],
            send_sem=gather_send.at[step - 1],
            recv_sem=gather_recv.at[step - 1],
            device_id=col_peer(step),
            device_id_type=MESH,
        )
        for step in range(1, col_size)
    ]

    for third in range(3):
        loads[2 + third].wait()
        bias = qkv_bias[pl.ds(third * width, width)].astype(F32).reshape(1, -1)
        part = (dot(normed[...], qkv_weight[third][...]) + bias).astype(BF16)
        packed[:, thirds[third]] = part * BF16(0.125) if third == 0 else part
        if third == 0:
            pl.semaphore_wait(barrier, col_size + dp_size - 2)
            for gather in gathers:
                gather.start()

    for gather in gathers:
        gather.wait()

    def forward_step(seq, carry):
        attention_forward(seq, width, packed, prefix, attended, top, bottom, side)
        return carry

    lax.fori_loop(0, seqs, forward_step, 0)

    loads[5].wait()
    bias = row(out_bias)
    gain_two, shift_two = row(ln2_gain), row(ln2_shift)

    def output_rows(block, rows):
        total = tokens[rows, :].astype(F32) + dot(attended[rows, :], out_weight[...]) + bias
        middle[rows, :] = total.astype(BF16)
        unit, _ = normalise(total)
        normed[rows, :] = (unit * gain_two + shift_two).astype(BF16)

    over_rows(row_count, GROUP, output_rows)

    for load in loads[6:]:
        load.wait()

    def ff_step(chunk, carry):
        units = pl.ds(pl.multiple_of(chunk * FF_CHUNK, FF_CHUNK), FF_CHUNK)
        bias = ff_bias[:, units]
        for start in range(0, row_count, FF_ROWS):
            rows = pl.ds(start, FF_ROWS)
            pre_act = dot(normed[rows, :], fc_weight[:, units]) + bias
            upstream = dot(stream[rows, :], proj_weight[units, :], NT)
            value, slope = gelu_and_slope(pre_act)
            activated[rows, units] = value.astype(BF16)
            wide[rows, units] = (slope * upstream).astype(BF16)
        return carry

    lax.fori_loop(0, ff // FF_CHUNK, ff_step, 0)

    def middle_rows(block, rows):
        upstream = dot(wide[rows, :], fc_weight[...], NT)
        total = stream[rows, :].astype(F32) + norm_pull(
            middle[rows, :].astype(F32), gain_two, upstream
        )
        low = total.astype(BF16)
        stream[rows, :] = low
        normed[rows, :] = dot(low, out_weight[...], NT).astype(BF16)

    over_rows(row_count, GROUP, middle_rows)

    reloads = [
        pltpu.make_async_copy(source, target, load_sem.at[place])
        for place, (source, target) in enumerate(
            [(tokens_hbm, tokens)]
            + [(qkv_hbm.at[:, thirds[third]], qkv_weight[third]) for third in range(3)]
        )
    ]
    for load in reloads:
        load.start()

    prefix_grad[...] = jnp.zeros_like(prefix_grad)

    def backward_step(seq, carry):
        attention_backward(
            seq, width, packed, prefix, normed, attended, top, bottom, side, prefix_grad
        )
        return carry

    lax.fori_loop(0, seqs, backward_step, 0)

    scatters = [
        pltpu.make_async_remote_copy(
            src_ref=prefix_grad.at[
                :, pl.ds(pl.multiple_of(lax.rem(my_col + step, col_size) * owned, PAIR), owned)
            ],
            dst_ref=parts_col.at[step - 1],
            send_sem=scatter_send.at[step - 1],
            recv_sem=scatter_recv.at[step - 1],
            device_id=col_peer(step),
            device_id_type=MESH,
        )
        for step in range(1, col_size)
    ]
    reduces = [
        pltpu.make_async_remote_copy(
            src_ref=parts_dp.at[my_dp],
            dst_ref=parts_dp.at[my_dp],
            send_sem=reduce_send.at[step - 1],
            recv_sem=reduce_recv.at[step - 1],
            device_id=dp_peer(step),
            device_id_type=MESH,
        )
        for step in range(1, dp_size)
    ]
    hiddens = [
        pltpu.make_async_remote_copy(
            src_ref=parts_hidden.at[my_col],
            dst_ref=parts_hidden.at[my_col],
            send_sem=hidden_send.at[step - 1],
            recv_sem=hidden_recv.at[step - 1],
            device_id=col_peer(step),
            device_id_type=MESH,
        )
        for step in range(1, col_size)
    ]

    def exchange(stage):
        if stage == 0:
            for scatter in scatters:
                scatter.start()
        elif stage == 1:
            for scatter in scatters:
                scatter.wait()
            total = prefix_grad[:, mine]
            for step in range(1, col_size):
                total = total + parts_col[step - 1]
            parts_dp[my_dp] = total
            for reduce in reduces:
                reduce.start()
        elif stage == 2:
            for reduce in reduces:
                reduce.wait()
            total = parts_dp[0]
            for step in range(1, dp_size):
                total = total + parts_dp[step]
            low = total.astype(BF16)
            owned_out[...] = low
            parts_hidden[my_col] = dot(low, second_weight[...], NT)
            for part in hiddens:
                part.start()
        else:
            for part in hiddens:
                part.wait()
            total = parts_hidden[0]
            for step in range(1, col_size):
                total = total + parts_hidden[step]
            first_weight_sum = hidden_full * hidden_full
            pre_out[...] = (total * (1.0 - first_weight_sum)).astype(BF16)

    exchange(0)
    proj_row = row(proj_bias)

    def proj_rows(block, rows):
        total = middle[rows, :].astype(F32) + dot(activated[rows, :], proj_weight[...]) + proj_row
        attended[rows, :] = total.astype(BF16)
        pl.when(block == 1)(lambda: exchange(1))

    over_rows(row_count, 1, proj_rows)
    for load in reloads:
        load.wait()

    def grad_rows(block, rows):
        upstream = dot(packed[rows, :], wide[0:width, 0 : 3 * width], NT)
        total = stream[rows, :].astype(F32) + norm_pull(
            tokens[rows, :].astype(F32), gain_one, upstream
        )
        stream[rows, :] = total.astype(BF16)
        pl.when(block == 1)(lambda: exchange(2))

    over_rows(row_count, 2, grad_rows)
    exchange(3)

def small_kernel(
    block_in,
    grad_in,
    hidden,
    owned,
    pre,
    embedding,
    first_hbm,
    block_out,
    grad_out,
    embed_grad,
    first_out,
    first_bias_grad,
    second_out,
    second_bias_grad,
    first_weight,
    first_grad,
    second_grad,
    sem,
):
    load = pltpu.make_async_copy(first_hbm, first_weight, sem.at[0])
    writes = [
        pltpu.make_async_copy(source, target, sem.at[1 + place])
        for place, (source, target) in enumerate(
            [
                (first_grad, first_out),
                (second_grad, second_out),
                (block_in, block_out),
                (grad_in, grad_out),
            ]
        )
    ]
    load.start()
    writes[2].start()
    writes[3].start()
    second_grad[...] = dot(hidden[...], owned[...], TN)
    writes[1].start()
    first_grad[...] = dot(embedding[...], pre[...], TN)
    writes[0].start()
    first_bias_grad[...] = jnp.sum(pre[...].astype(F32), axis=0)
    second_bias_grad[...] = jnp.sum(owned[...].astype(F32), axis=0)
    load.wait()
    embed_grad[...] = dot(pre[...], first_weight[...], NT)[:PREFIX]
    for write in writes:
        write.wait()


def shards(
    dp_size,
    col_size,
    tokens,
    cotangent,
    ln1_gain,
    ln1_shift,
    qkv_weight,
    qkv_bias,
    out_weight,
    out_bias,
    ln2_gain,
    ln2_shift,
    fc_weight,
    fc_bias,
    proj_weight,
    proj_bias,
    embedding,
    first_weight,
    first_bias,
    second_weight,
    second_bias,
):
    row_count, width = tokens.shape
    ff = fc_weight.shape[1]
    hidden_width, owned = second_weight.shape
    heads = row_count // SEQ_LEN * HEADS
    anywhere = pl.BlockSpec(memory_space=pl.ANY)
    local = pl.BlockSpec(memory_space=pltpu.VMEM)
    dma = pltpu.SemaphoreType.DMA
    results = pl.pallas_call(
        functools.partial(layer_kernel, dp_size, col_size),
        out_shape=(
            pltpu.VMEM((row_count, width), BF16),
            pltpu.VMEM((row_count, width), BF16),
            pltpu.VMEM((PAD, hidden_width), BF16),
            pltpu.VMEM((PAD, owned), BF16),
            pltpu.VMEM((PAD, hidden_width), BF16),
            pltpu.VMEM((PAD, width), BF16),
        ),
        in_specs=[anywhere] * 8 + [local] * 11,
        out_specs=[local] * 6,
        scratch_shapes=[
            pltpu.VMEM((max(row_count, width), ff), BF16),
            pltpu.VMEM((width, width), BF16),
            pltpu.VMEM((width, ff), BF16),
            pltpu.VMEM((ff, width), BF16),
            pltpu.VMEM((row_count, 3 * width), BF16),
            pltpu.VMEM((heads, HALF, SEQ_LEN), BF16),
            pltpu.VMEM((heads, HALF, HALF), BF16),
            pltpu.VMEM((heads, PAD, SEQ_LEN), BF16),
            pltpu.VMEM((row_count, width), BF16),
            pltpu.VMEM((row_count, width), BF16),
            pltpu.VMEM((max(row_count, width), ff), BF16),
            pltpu.VMEM((hidden_width, owned), BF16),
            pltpu.VMEM((PAD, col_size * owned), BF16),
            pltpu.VMEM((PAD, col_size * owned), F32),
            pltpu.VMEM((PAD, width), F32),
            pltpu.VMEM((1, ff), F32),
            pltpu.VMEM((col_size - 1, PAD, owned), F32),
            pltpu.VMEM((dp_size, PAD, owned), F32),
            pltpu.VMEM((col_size, PAD, hidden_width), F32),
            dma((9 + row_count // BLOCK,)),
            dma((col_size - 1,)),
            dma((col_size - 1,)),
            dma((col_size - 1,)),
            dma((col_size - 1,)),
            dma((dp_size - 1,)),
            dma((dp_size - 1,)),
            dma((col_size - 1,)),
            dma((col_size - 1,)),
        ],
        compiler_params=pltpu.CompilerParams(
            collective_id=0, has_side_effects=True, vmem_limit_bytes=239 * 2**18
        ),
        name="layer",
    )(
        tokens,
        cotangent,
        qkv_weight,
        out_weight,
        fc_weight,
        proj_weight,
        first_weight,
        second_weight,
        ln1_gain,
        ln1_shift,
        qkv_bias,
        out_bias,
        ln2_gain,
        ln2_shift,
        fc_bias,
        proj_bias,
        embedding,
        first_bias,
        second_bias,
    )
    held = [pltpu.with_memory_space_constraint(result, pltpu.VMEM) for result in results]
    return pl.pallas_call(
        small_kernel,
        out_shape=(
            jax.ShapeDtypeStruct((row_count, width), BF16),
            jax.ShapeDtypeStruct((row_count, width), BF16),
            jax.ShapeDtypeStruct((PREFIX, width), F32),
            jax.ShapeDtypeStruct((width, hidden_width), F32),
            jax.ShapeDtypeStruct((hidden_width,), F32),
            jax.ShapeDtypeStruct((hidden_width, owned), F32),
            jax.ShapeDtypeStruct((owned,), F32),
        ),
        in_specs=[local] * 6 + [anywhere],
        out_specs=[anywhere, anywhere, local, anywhere, local, anywhere, local],
        scratch_shapes=[
            pltpu.VMEM((width, hidden_width), BF16),
            pltpu.VMEM((width, hidden_width), F32),
            pltpu.VMEM((hidden_width, owned), F32),
            dma((5,)),
        ],
        compiler_params=pltpu.CompilerParams(vmem_limit_bytes=16 * 2**20),
        name="small_grads",
    )(*held, first_weight)


def solution(mesh):
    placed = (
        P(("dp", "col"), None),
        P(("dp", "col"), None),
        P(),
        P(),
        P(),
        P(),
        P(),
        P(),
        P(),
        P(),
        P(),
        P(),
        P(),
        P(),
        P(),
        P(),
        P(),
        P(None, "col"),
        P("col"),
    )
    return jax.shard_map(
        functools.partial(shards, mesh.shape["dp"], mesh.shape["col"]),
        mesh=mesh,
        in_specs=placed,
        out_specs=(
            P(("dp", "col"), None),
            P(("dp", "col"), None),
            P(),
            P(),
            P(),
            P(None, "col"),
            P("col"),
        ),
        check_vma=False,
    )
```

```python
import functools

import jax
import jax.numpy as jnp
from jax import lax
from jax.experimental import pallas as pl
from jax.experimental.pallas import tpu as pltpu
from jax.sharding import PartitionSpec as P

HEADS = 16
PREFIX = 10
PAD = 16
SEQ_LEN = 256
HALF = SEQ_LEN // 2
PAIR = 128
BLOCK = 256
FF_CHUNK = 512
FF_ROWS = 1024
GROUP = 2

EPSILON = 1e-05
MASKED = -1000000000.0
NEVER = -1e30
ROOT = 0.7978845608028654
CUBIC = 0.044715

F32 = jnp.float32
BF16 = jnp.bfloat16
NN = (((1,), (0,)), ((), ()))
NT = (((1,), (1,)), ((), ()))
TN = (((0,), (0,)), ((), ()))
MESH = pl.DeviceIdType.MESH


def dot(left, right, form=NN):
    return lax.dot_general(left, right, form, preferred_element_type=F32)


def row(ref):
    return ref[...].astype(F32).reshape(1, -1)


def centre(values):
    average = jnp.mean(values, axis=-1, keepdims=True)
    centred = values - average
    variance = jnp.mean(centred * centred, axis=-1, keepdims=True)
    return centred, lax.rsqrt(variance + EPSILON)


def normalise(values):
    centred, scale = centre(values)
    return centred * scale


def norm_pull(values, gain, upstream):
    centred, scale = centre(values)
    scaled = upstream * gain
    first = jnp.mean(scaled, axis=-1, keepdims=True)
    second = jnp.mean(scaled * centred, axis=-1, keepdims=True)
    return (scaled - first) * scale - centred * (scale * scale * scale * second)


def gelu_and_slope(values):
    square = values * values
    inner = jnp.tanh(values * (ROOT + (ROOT * CUBIC) * square))
    half = 0.5 * inner + 0.5
    bend = (0.5 - 0.5 * inner * inner) * (ROOT + (3.0 * ROOT * CUBIC) * square)
    return values * half, half + values * bend


def head_lanes():
    lane = lax.broadcasted_iota(jnp.int32, (1, PAIR), 1)
    return (lane < PAIR // 2, lane >= PAIR // 2)


def columns(base, pair):
    return pl.ds(base + pair * PAIR, PAIR)


def over_rows(row_count, group, body):
    def step(index, carry):
        for place in range(group):
            block = index * group + place
            body(block, pl.ds(pl.multiple_of(block * BLOCK, BLOCK), BLOCK))
        return carry

    lax.fori_loop(0, row_count // (BLOCK * group), step, 0)


def pair_products(mine, prefix, others, lanes):
    stacked = [jnp.where(lane, mine[:HALF], 0) for lane in lanes]
    stacked += [jnp.where(lane, prefix, 0) for lane in lanes]
    late = jnp.concatenate([jnp.where(lane, others[HALF:], 0) for lane in lanes], axis=0)
    second = dot(mine[HALF:], late, NT)
    rest = dot(jnp.concatenate(stacked, axis=0), others, NT)
    return [
        (
            rest[head * HALF : (head + 1) * HALF],
            second[:, head * HALF : (head + 1) * HALF],
            rest[2 * HALF + head * PAD : 2 * HALF + (head + 1) * PAD],
        )
        for head in (0, 1)
    ]


def attention_forward(seq, width, packed, prefix, attended, top, bottom, side):
    rows = pl.ds(pl.multiple_of(seq * SEQ_LEN, SEQ_LEN), SEQ_LEN)
    pairs = width // PAIR
    key = lax.broadcasted_iota(jnp.int32, (HALF, HALF), 0)
    query = lax.broadcasted_iota(jnp.int32, (HALF, HALF), 1)
    causal = key <= query
    real = lax.broadcasted_iota(jnp.int32, (PAD, 1), 0) < PREFIX
    lanes = head_lanes()
    scores = []
    for pair in range(pairs):
        scores += pair_products(
            packed[rows, columns(width, pair)],
            prefix[:, columns(0, pair)],
            packed[rows, columns(0, pair)],
            lanes,
        )
    probs = []
    for first, second, extra in scores:
        extra = jnp.where(real, extra, NEVER)
        early = jnp.where(causal, first[:, :HALF], MASKED)
        cross = first[:, HALF:]
        late = jnp.where(causal, second, MASKED)
        peak = jnp.max(extra, axis=0, keepdims=True)
        peak_early = jnp.maximum(jnp.max(early, axis=0, keepdims=True), peak[:, :HALF])
        peak_late = jnp.maximum(
            jnp.maximum(
                jnp.max(cross, axis=0, keepdims=True), jnp.max(late, axis=0, keepdims=True)
            ),
            peak[:, HALF:],
        )
        early = jnp.exp(early - peak_early)
        cross = jnp.exp(cross - peak_late)
        late = jnp.exp(late - peak_late)
        extra = jnp.exp(extra - jnp.concatenate([peak_early, peak_late], axis=1))
        total = jnp.sum(extra, axis=0, keepdims=True)
        total_early = jnp.sum(early, axis=0, keepdims=True) + total[:, :HALF]
        total_late = (
            jnp.sum(cross, axis=0, keepdims=True)
            + jnp.sum(late, axis=0, keepdims=True)
            + total[:, HALF:]
        )
        inverse = 1.0 / jnp.concatenate([total_early, total_late], axis=1)
        first = jnp.concatenate(
            [
                (early * inverse[:, :HALF]).astype(BF16),
                (cross * inverse[:, HALF:]).astype(BF16),
            ],
            axis=1,
        )
        probs.append(
            (first, (late * inverse[:, HALF:]).astype(BF16), (extra * inverse).astype(BF16))
        )
    empty = jnp.zeros((HALF, HALF), BF16)
    for pair in range(pairs):
        values = packed[rows, columns(2 * width, pair)].T
        prefix_values = prefix[:, columns(width, pair)].T
        halves = []
        for head in (0, 1):
            first, second, extra = probs[2 * pair + head]
            place = seq * HEADS + 2 * pair + head
            top[place] = first
            bottom[place] = second
            side[place] = extra
            whole = jnp.concatenate([first, jnp.concatenate([empty, second], axis=1)], axis=0)
            mine = slice(head * (PAIR // 2), (head + 1) * (PAIR // 2))
            halves.append(dot(values[mine], whole) + dot(prefix_values[mine], extra))
        attended[rows, columns(0, pair)] = jnp.concatenate(halves, axis=0).astype(BF16).T


def attention_backward(
    seq, width, packed, prefix, upstream, attended, top, bottom, side, prefix_grad
):
    rows = pl.ds(pl.multiple_of(seq * SEQ_LEN, SEQ_LEN), SEQ_LEN)
    pairs = width // PAIR
    lanes = head_lanes()
    head_row = lax.broadcasted_iota(jnp.int32, (8, PAIR), 0)
    head_lane = lax.broadcasted_iota(jnp.int32, (8, PAIR), 1)
    picker = jnp.where(head_lane // (PAIR // 2) == head_row, 1.0, 0.0).astype(BF16)
    empty = jnp.zeros((HALF, HALF), BF16)
    incoming, deltas = [], []
    for pair in range(pairs):
        grad = upstream[rows, columns(0, pair)]
        deltas.append(dot(picker, grad * attended[rows, columns(0, pair)], NT))
        incoming.append(
            pair_products(
                packed[rows, columns(2 * width, pair)], prefix[:, columns(width, pair)], grad, lanes
            )
        )
    slopes = []
    for pair in range(pairs):
        for head in (0, 1):
            place = seq * HEADS + 2 * pair + head
            first, second, extra = incoming[pair][head]
            delta = deltas[pair][head : head + 1, :]
            first = (top[place].astype(F32) * (first - delta)).astype(BF16)
            second = (bottom[place].astype(F32) * (second - delta[:, HALF:])).astype(BF16)
            extra = (side[place].astype(F32) * (extra - delta)).astype(BF16)
            slopes.append((first, second, extra))
    for pair in range(pairs):
        grad = upstream[rows, columns(0, pair)]
        queries = packed[rows, columns(0, pair)]
        keys = packed[rows, columns(width, pair)].T
        prefix_keys = prefix[:, columns(0, pair)].T
        place = seq * HEADS + 2 * pair

        def pulled(stream, first, second, extra):
            masked = [jnp.where(mine, stream, 0) for mine in lanes]
            both = jnp.concatenate(masked, axis=0)
            late = jnp.concatenate([part[HALF:] for part in masked], axis=0)
            joined = [jnp.concatenate(part, axis=1) for part in (first, second)]
            beside = dot(jnp.concatenate(extra, axis=0), stream)
            beside = jnp.where(lanes[0], beside[:PAD], beside[PAD:])
            return dot(joined[0], both), dot(joined[1], late), beside

        left, right = slopes[2 * pair], slopes[2 * pair + 1]
        key_first, key_second, key_extra = pulled(
            queries, (left[0], right[0]), (left[1], right[1]), (left[2], right[2])
        )
        value_first, value_second, value_extra = pulled(
            grad,
            (top[place], top[place + 1]),
            (bottom[place], bottom[place + 1]),
            (side[place], side[place + 1]),
        )
        halves = []
        for head in (0, 1):
            first, second, extra = slopes[2 * pair + head]
            whole = jnp.concatenate([first, jnp.concatenate([empty, second], axis=1)], axis=0)
            mine = slice(head * (PAIR // 2), (head + 1) * (PAIR // 2))
            halves.append(dot(keys[mine], whole) + dot(prefix_keys[mine], extra))
        prefix_grad[:, columns(0, pair)] += key_extra
        prefix_grad[:, columns(width, pair)] += value_extra
        packed[rows, columns(0, pair)] = (
            (jnp.concatenate(halves, axis=0) * 0.125).astype(BF16).T
        )
        packed[rows, columns(width, pair)] = jnp.concatenate(
            [key_first, key_second], axis=0
        ).astype(BF16)
        packed[rows, columns(2 * width, pair)] = jnp.concatenate(
            [value_first, value_second], axis=0
        ).astype(BF16)


def layer_kernel(
    dp_size,
    col_size,
    tokens_hbm,
    cotangent_hbm,
    qkv_hbm,
    out_hbm,
    fc_hbm,
    proj_hbm,
    first_hbm,
    second_hbm,
    ln1_gain,
    ln1_shift,
    qkv_bias,
    out_bias,
    ln2_gain,
    ln2_shift,
    fc_bias,
    proj_bias,
    embedding,
    first_bias,
    second_bias,
    attended,
    stream,
    hidden_out,
    owned_out,
    pre_out,
    embed_out,
    wide,
    out_weight,
    fc_weight,
    proj_weight,
    packed,
    top,
    bottom,
    side,
    middle,
    normed,
    activated,
    second_weight,
    prefix,
    prefix_grad,
    padded,
    ff_bias,
    parts_col,
    parts_dp,
    parts_hidden,
    load_sem,
    gather_send,
    gather_recv,
    scatter_send,
    scatter_recv,
    reduce_send,
    reduce_recv,
    hidden_send,
    hidden_recv,
):
    row_count, width = stream.shape
    ff = activated.shape[1]
    tokens = wide.at[pl.ds(0, row_count), pl.ds(3 * width, width)]
    hidden_width = second_weight.shape[0]
    owned = second_weight.shape[1]
    seqs = row_count // SEQ_LEN
    my_dp = lax.axis_index("dp")
    my_col = lax.axis_index("col")

    def col_peer(step):
        return (my_dp, lax.rem(my_col + step, col_size))

    def dp_peer(step):
        return (lax.rem(my_dp + step, dp_size), my_col)

    barrier = pltpu.get_barrier_semaphore()
    for step in range(1, col_size):
        pl.semaphore_signal(barrier, inc=1, device_id=col_peer(step), device_id_type=MESH)
    for step in range(1, dp_size):
        pl.semaphore_signal(barrier, inc=1, device_id=dp_peer(step), device_id_type=MESH)

    first_weight = activated.at[pl.ds(0, width), pl.ds(0, hidden_width)]
    thirds = [pl.ds(third * width, width) for third in range(3)]
    qkv_weight = [wide.at[pl.ds(0, width), third] for third in thirds]
    blocks = row_count // BLOCK
    block_rows = [pl.ds(block * BLOCK, BLOCK) for block in range(blocks)]
    loads = [
        pltpu.make_async_copy(source, target, load_sem.at[place])
        for place, (source, target) in enumerate(
            [(tokens_hbm.at[rows, :], tokens.at[rows, :]) for rows in block_rows]
            + [(first_hbm, first_weight), (second_hbm, second_weight)]
            + [(qkv_hbm.at[:, thirds[third]], qkv_weight[third]) for third in range(3)]
            + [
                (out_hbm, out_weight),
                (fc_hbm, fc_weight),
                (proj_hbm, proj_weight),
                (cotangent_hbm, stream),
            ]
        )
    ]
    for load in loads:
        load.start()
    token_loads, loads = loads[:blocks], loads[blocks:]

    padded[...] = jnp.zeros_like(padded)
    padded[0:PREFIX, :] = embedding[...].astype(F32)
    ff_bias[...] = row(fc_bias)

    gain_one, shift_one = row(ln1_gain), row(ln1_shift)
    for load, rows in zip(token_loads, block_rows):
        load.wait()
        unit = normalise(tokens[rows, :].astype(F32))
        normed[rows, :] = (unit * gain_one + shift_one).astype(BF16)

    loads[0].wait()
    loads[1].wait()
    embed_out[...] = padded[...].astype(BF16)
    pre_hidden = dot(embed_out[...], first_weight[...]) + row(first_bias)
    hidden_full = jnp.tanh(pre_hidden)
    hidden_low = hidden_full.astype(BF16)
    hidden_out[...] = hidden_low
    owned_kv = dot(hidden_low, second_weight[...]) + row(second_bias)
    mine = pl.ds(pl.multiple_of(my_col * owned, PAIR), owned)
    prefix[:, mine] = owned_kv.astype(BF16)
    gathers = [
        pltpu.make_async_remote_copy(
            src_ref=prefix.at[:, mine],
            dst_ref=prefix.at[:, mine],
            send_sem=gather_send.at[step - 1],
            recv_sem=gather_recv.at[step - 1],
            device_id=col_peer(step),
            device_id_type=MESH,
        )
        for step in range(1, col_size)
    ]

    for third in range(3):
        loads[2 + third].wait()
        bias = qkv_bias[pl.ds(third * width, width)].astype(F32).reshape(1, -1)
        part = (dot(normed[...], qkv_weight[third][...]) + bias).astype(BF16)
        packed[:, thirds[third]] = part * BF16(0.125) if third == 0 else part
        if third == 0:
            pl.semaphore_wait(barrier, col_size + dp_size - 2)
            for gather in gathers:
                gather.start()

    for gather in gathers:
        gather.wait()

    def forward_step(seq, carry):
        attention_forward(seq, width, packed, prefix, attended, top, bottom, side)
        return carry

    lax.fori_loop(0, seqs, forward_step, 0)

    loads[5].wait()
    bias = row(out_bias)
    gain_two, shift_two = row(ln2_gain), row(ln2_shift)

    def output_rows(block, rows):
        total = tokens[rows, :].astype(F32) + dot(attended[rows, :], out_weight[...]) + bias
        middle[rows, :] = total.astype(BF16)
        unit = normalise(total)
        normed[rows, :] = (unit * gain_two + shift_two).astype(BF16)

    over_rows(row_count, 4, output_rows)

    for load in loads[6:]:
        load.wait()

    def ff_step(chunk, carry):
        units = pl.ds(pl.multiple_of(chunk * FF_CHUNK, FF_CHUNK), FF_CHUNK)
        bias = ff_bias[:, units]
        for start in range(0, row_count, FF_ROWS):
            rows = pl.ds(start, FF_ROWS)
            pre_act = dot(normed[rows, :], fc_weight[:, units]) + bias
            upstream = dot(stream[rows, :], proj_weight[units, :], NT)
            value, slope = gelu_and_slope(pre_act)
            activated[rows, units] = value.astype(BF16)
            wide[rows, units] = (slope * upstream).astype(BF16)
        return carry

    lax.fori_loop(0, ff // FF_CHUNK, ff_step, 0)

    def middle_rows(block, rows):
        upstream = dot(wide[rows, :], fc_weight[...], NT)
        total = stream[rows, :].astype(F32) + norm_pull(
            middle[rows, :].astype(F32), gain_two, upstream
        )
        low = total.astype(BF16)
        stream[rows, :] = low
        normed[rows, :] = dot(low, out_weight[...], NT).astype(BF16)

    over_rows(row_count, 4, middle_rows)

    reloads = [
        pltpu.make_async_copy(source, target, load_sem.at[place])
        for place, (source, target) in enumerate(
            [(tokens_hbm, tokens)]
            + [(qkv_hbm.at[:, thirds[third]], qkv_weight[third]) for third in range(3)]
        )
    ]
    for load in reloads:
        load.start()

    prefix_grad[...] = jnp.zeros_like(prefix_grad)

    def backward_step(seq, carry):
        attention_backward(
            seq, width, packed, prefix, normed, attended, top, bottom, side, prefix_grad
        )
        return carry

    lax.fori_loop(0, seqs, backward_step, 0)

    scatters = [
        pltpu.make_async_remote_copy(
            src_ref=prefix_grad.at[
                :, pl.ds(pl.multiple_of(lax.rem(my_col + step, col_size) * owned, PAIR), owned)
            ],
            dst_ref=parts_col.at[step - 1],
            send_sem=scatter_send.at[step - 1],
            recv_sem=scatter_recv.at[step - 1],
            device_id=col_peer(step),
            device_id_type=MESH,
        )
        for step in range(1, col_size)
    ]
    reduces = [
        pltpu.make_async_remote_copy(
            src_ref=parts_dp.at[my_dp],
            dst_ref=parts_dp.at[my_dp],
            send_sem=reduce_send.at[step - 1],
            recv_sem=reduce_recv.at[step - 1],
            device_id=dp_peer(step),
            device_id_type=MESH,
        )
        for step in range(1, dp_size)
    ]
    hiddens = [
        pltpu.make_async_remote_copy(
            src_ref=parts_hidden.at[my_col],
            dst_ref=parts_hidden.at[my_col],
            send_sem=hidden_send.at[step - 1],
            recv_sem=hidden_recv.at[step - 1],
            device_id=col_peer(step),
            device_id_type=MESH,
        )
        for step in range(1, col_size)
    ]

    def exchange(stage):
        if stage == 0:
            for scatter in scatters:
                scatter.start()
        elif stage == 1:
            for scatter in scatters:
                scatter.wait()
            total = prefix_grad[:, mine]
            for step in range(1, col_size):
                total = total + parts_col[step - 1]
            parts_dp[my_dp] = total
            for reduce in reduces:
                reduce.start()
        elif stage == 2:
            for reduce in reduces:
                reduce.wait()
            total = parts_dp[0]
            for step in range(1, dp_size):
                total = total + parts_dp[step]
            low = total.astype(BF16)
            owned_out[...] = low
            parts_hidden[my_col] = dot(low, second_weight[...], NT)
            for part in hiddens:
                part.start()
        else:
            for part in hiddens:
                part.wait()
            total = parts_hidden[0]
            for step in range(1, col_size):
                total = total + parts_hidden[step]
            first_weight_sum = hidden_full * hidden_full
            pre_out[...] = (total * (1.0 - first_weight_sum)).astype(BF16)

    exchange(0)
    proj_row = row(proj_bias)

    def proj_rows(block, rows):
        total = middle[rows, :].astype(F32) + dot(activated[rows, :], proj_weight[...]) + proj_row
        attended[rows, :] = total.astype(BF16)
        pl.when(block == 1)(lambda: exchange(1))

    over_rows(row_count, 2, proj_rows)
    for load in reloads:
        load.wait()

    def grad_rows(block, rows):
        upstream = dot(packed[rows, :], wide[0:width, 0 : 3 * width], NT)
        total = stream[rows, :].astype(F32) + norm_pull(
            tokens[rows, :].astype(F32), gain_one, upstream
        )
        stream[rows, :] = total.astype(BF16)
        pl.when(block == 1)(lambda: exchange(2))

    over_rows(row_count, 2, grad_rows)
    exchange(3)

def small_kernel(
    block_in,
    grad_in,
    hidden,
    owned,
    pre,
    embedding,
    first_hbm,
    block_out,
    grad_out,
    embed_out,
    first_out,
    first_bias_out,
    second_out,
    second_bias_out,
    first_weight,
    first_grad,
    second_grad,
    first_bias_grad,
    second_bias_grad,
    embed_grad,
    sem,
):
    load = pltpu.make_async_copy(first_hbm, first_weight, sem.at[0])
    writes = [
        pltpu.make_async_copy(source, target, sem.at[1 + place])
        for place, (source, target) in enumerate(
            [
                (block_in, block_out),
                (grad_in, grad_out),
                (second_grad, second_out),
                (first_grad, first_out),
                (first_bias_grad, first_bias_out),
                (second_bias_grad, second_bias_out),
                (embed_grad, embed_out),
            ]
        )
    ]
    load.start()
    writes[0].start()
    writes[1].start()
    second_grad[...] = dot(hidden[...], owned[...], TN)
    writes[2].start()
    first_grad[...] = dot(embedding[...], pre[...], TN)
    writes[3].start()
    first_bias_grad[...] = jnp.sum(pre[...].astype(F32), axis=0)
    writes[4].start()
    second_bias_grad[...] = jnp.sum(owned[...].astype(F32), axis=0)
    writes[5].start()
    load.wait()
    embed_grad[...] = dot(pre[...], first_weight[...], NT)[:PREFIX]
    writes[6].start()
    for write in writes:
        write.wait()


def shards(
    dp_size,
    col_size,
    tokens,
    cotangent,
    ln1_gain,
    ln1_shift,
    qkv_weight,
    qkv_bias,
    out_weight,
    out_bias,
    ln2_gain,
    ln2_shift,
    fc_weight,
    fc_bias,
    proj_weight,
    proj_bias,
    embedding,
    first_weight,
    first_bias,
    second_weight,
    second_bias,
):
    row_count, width = tokens.shape
    ff = fc_weight.shape[1]
    hidden_width, owned = second_weight.shape
    heads = row_count // SEQ_LEN * HEADS
    anywhere = pl.BlockSpec(memory_space=pl.ANY)
    local = pl.BlockSpec(memory_space=pltpu.VMEM)
    dma = pltpu.SemaphoreType.DMA
    results = pl.pallas_call(
        functools.partial(layer_kernel, dp_size, col_size),
        out_shape=(
            pltpu.VMEM((row_count, width), BF16),
            pltpu.VMEM((row_count, width), BF16),
            pltpu.VMEM((PAD, hidden_width), BF16),
            pltpu.VMEM((PAD, owned), BF16),
            pltpu.VMEM((PAD, hidden_width), BF16),
            pltpu.VMEM((PAD, width), BF16),
        ),
        in_specs=[anywhere] * 8 + [local] * 11,
        out_specs=[local] * 6,
        scratch_shapes=[
            pltpu.VMEM((max(row_count, width), ff), BF16),
            pltpu.VMEM((width, width), BF16),
            pltpu.VMEM((width, ff), BF16),
            pltpu.VMEM((ff, width), BF16),
            pltpu.VMEM((row_count, 3 * width), BF16),
            pltpu.VMEM((heads, HALF, SEQ_LEN), BF16),
            pltpu.VMEM((heads, HALF, HALF), BF16),
            pltpu.VMEM((heads, PAD, SEQ_LEN), BF16),
            pltpu.VMEM((row_count, width), BF16),
            pltpu.VMEM((row_count, width), BF16),
            pltpu.VMEM((max(row_count, width), ff), BF16),
            pltpu.VMEM((hidden_width, owned), BF16),
            pltpu.VMEM((PAD, col_size * owned), BF16),
            pltpu.VMEM((PAD, col_size * owned), F32),
            pltpu.VMEM((PAD, width), F32),
            pltpu.VMEM((1, ff), F32),
            pltpu.VMEM((col_size - 1, PAD, owned), F32),
            pltpu.VMEM((dp_size, PAD, owned), F32),
            pltpu.VMEM((col_size, PAD, hidden_width), F32),
            dma((9 + row_count // BLOCK,)),
            dma((col_size - 1,)),
            dma((col_size - 1,)),
            dma((col_size - 1,)),
            dma((col_size - 1,)),
            dma((dp_size - 1,)),
            dma((dp_size - 1,)),
            dma((col_size - 1,)),
            dma((col_size - 1,)),
        ],
        compiler_params=pltpu.CompilerParams(
            collective_id=0, has_side_effects=True, vmem_limit_bytes=239 * 2**18
        ),
        name="layer",
    )(
        tokens,
        cotangent,
        qkv_weight,
        out_weight,
        fc_weight,
        proj_weight,
        first_weight,
        second_weight,
        ln1_gain,
        ln1_shift,
        qkv_bias,
        out_bias,
        ln2_gain,
        ln2_shift,
        fc_bias,
        proj_bias,
        embedding,
        first_bias,
        second_bias,
    )
    held = [pltpu.with_memory_space_constraint(result, pltpu.VMEM) for result in results]
    return pl.pallas_call(
        small_kernel,
        out_shape=(
            jax.ShapeDtypeStruct((row_count, width), BF16),
            jax.ShapeDtypeStruct((row_count, width), BF16),
            jax.ShapeDtypeStruct((PREFIX, width), F32),
            jax.ShapeDtypeStruct((width, hidden_width), F32),
            jax.ShapeDtypeStruct((hidden_width,), F32),
            jax.ShapeDtypeStruct((hidden_width, owned), F32),
            jax.ShapeDtypeStruct((owned,), F32),
        ),
        in_specs=[local] * 6 + [anywhere],
        out_specs=[anywhere] * 7,
        scratch_shapes=[
            pltpu.VMEM((width, hidden_width), BF16),
            pltpu.VMEM((width, hidden_width), F32),
            pltpu.VMEM((hidden_width, owned), F32),
            pltpu.VMEM((hidden_width,), F32),
            pltpu.VMEM((owned,), F32),
            pltpu.VMEM((PREFIX, width), F32),
            dma((8,)),
        ],
        compiler_params=pltpu.CompilerParams(vmem_limit_bytes=16 * 2**20),
        name="small_grads",
    )(*held, first_weight)


def solution(mesh):
    placed = (
        P(("dp", "col"), None),
        P(("dp", "col"), None),
        P(),
        P(),
        P(),
        P(),
        P(),
        P(),
        P(),
        P(),
        P(),
        P(),
        P(),
        P(),
        P(),
        P(),
        P(),
        P(None, "col"),
        P("col"),
    )
    return jax.shard_map(
        functools.partial(shards, mesh.shape["dp"], mesh.shape["col"]),
        mesh=mesh,
        in_specs=placed,
        out_specs=(
            P(("dp", "col"), None),
            P(("dp", "col"), None),
            P(),
            P(),
            P(),
            P(None, "col"),
            P("col"),
        ),
        check_vma=False,
    )
```

```python
import functools

import jax
import jax.numpy as jnp
from jax import lax
from jax.experimental import pallas as pl
from jax.experimental.pallas import tpu as pltpu
from jax.sharding import PartitionSpec as P

HEADS = 16
PREFIX = 10
PAD = 16
SEQ_LEN = 256
HALF = SEQ_LEN // 2
PAIR = 128
BLOCK = 256
FF_CHUNK = 512
FF_ROWS = 1024
GROUP = 2

EPSILON = 1e-05
MASKED = -1000000000.0
NEVER = -1e30
ROOT = 0.7978845608028654
CUBIC = 0.044715

F32 = jnp.float32
BF16 = jnp.bfloat16
NN = (((1,), (0,)), ((), ()))
NT = (((1,), (1,)), ((), ()))
TN = (((0,), (0,)), ((), ()))
MESH = pl.DeviceIdType.MESH


def dot(left, right, form=NN):
    return lax.dot_general(left, right, form, preferred_element_type=F32)


def row(ref):
    return ref[...].astype(F32).reshape(1, -1)


def centre(values):
    average = jnp.mean(values, axis=-1, keepdims=True)
    centred = values - average
    variance = jnp.mean(centred * centred, axis=-1, keepdims=True)
    return centred, lax.rsqrt(variance + EPSILON)


def normalise(values):
    centred, scale = centre(values)
    return centred * scale


def norm_pull(values, gain, upstream):
    centred, scale = centre(values)
    scaled = upstream * gain
    first = jnp.mean(scaled, axis=-1, keepdims=True)
    second = jnp.mean(scaled * centred, axis=-1, keepdims=True)
    return (scaled - first) * scale - centred * (scale * scale * scale * second)


def gelu_and_slope(values):
    square = values * values
    inner = jnp.tanh(values * (ROOT + (ROOT * CUBIC) * square))
    half = 0.5 * inner + 0.5
    bend = (0.5 - 0.5 * inner * inner) * (ROOT + (3.0 * ROOT * CUBIC) * square)
    return values * half, half + values * bend


def head_lanes():
    lane = lax.broadcasted_iota(jnp.int32, (1, PAIR), 1)
    return (lane < PAIR // 2, lane >= PAIR // 2)


def columns(base, pair):
    return pl.ds(base + pair * PAIR, PAIR)


def over_rows(row_count, group, body):
    def step(index, carry):
        for place in range(group):
            block = index * group + place
            body(block, pl.ds(pl.multiple_of(block * BLOCK, BLOCK), BLOCK))
        return carry

    lax.fori_loop(0, row_count // (BLOCK * group), step, 0)


def pair_products(mine, prefix, others, lanes):
    stacked = [jnp.where(lane, mine[:HALF], 0) for lane in lanes]
    stacked += [jnp.where(lane, prefix, 0) for lane in lanes]
    late = jnp.concatenate([jnp.where(lane, others[HALF:], 0) for lane in lanes], axis=0)
    second = dot(mine[HALF:], late, NT)
    rest = dot(jnp.concatenate(stacked, axis=0), others, NT)
    return [
        (
            rest[head * HALF : (head + 1) * HALF],
            second[:, head * HALF : (head + 1) * HALF],
            rest[2 * HALF + head * PAD : 2 * HALF + (head + 1) * PAD],
        )
        for head in (0, 1)
    ]


def attention_forward(seq, width, packed, prefix, attended, top, bottom, side, norms):
    rows = pl.ds(pl.multiple_of(seq * SEQ_LEN, SEQ_LEN), SEQ_LEN)
    pairs = width // PAIR
    key = lax.broadcasted_iota(jnp.int32, (HALF, HALF), 0)
    query = lax.broadcasted_iota(jnp.int32, (HALF, HALF), 1)
    causal = key <= query
    real = lax.broadcasted_iota(jnp.int32, (PAD, 1), 0) < PREFIX
    lanes = head_lanes()
    scores = []
    for pair in range(pairs):
        scores += pair_products(
            packed[rows, columns(width, pair)],
            prefix[:, columns(0, pair)],
            packed[rows, columns(0, pair)],
            lanes,
        )
    probs = []
    for first, second, extra in scores:
        extra = jnp.where(real, extra, NEVER)
        early = jnp.where(causal, first[:, :HALF], MASKED)
        cross = first[:, HALF:]
        late = jnp.where(causal, second, MASKED)
        peak = jnp.max(extra, axis=0, keepdims=True)
        peak_early = jnp.maximum(jnp.max(early, axis=0, keepdims=True), peak[:, :HALF])
        peak_late = jnp.maximum(
            jnp.maximum(
                jnp.max(cross, axis=0, keepdims=True), jnp.max(late, axis=0, keepdims=True)
            ),
            peak[:, HALF:],
        )
        early = jnp.exp(early - peak_early)
        cross = jnp.exp(cross - peak_late)
        late = jnp.exp(late - peak_late)
        extra = jnp.exp(extra - jnp.concatenate([peak_early, peak_late], axis=1))
        total = jnp.sum(extra, axis=0, keepdims=True)
        total_early = jnp.sum(early, axis=0, keepdims=True) + total[:, :HALF]
        total_late = (
            jnp.sum(cross, axis=0, keepdims=True)
            + jnp.sum(late, axis=0, keepdims=True)
            + total[:, HALF:]
        )
        inverse = 1.0 / jnp.concatenate([total_early, total_late], axis=1)
        first = jnp.concatenate([early.astype(BF16), cross.astype(BF16)], axis=1)
        probs.append((first, late.astype(BF16), extra.astype(BF16), inverse))
    empty = jnp.zeros((HALF, HALF), BF16)
    for pair in range(pairs):
        values = packed[rows, columns(2 * width, pair)].T
        prefix_values = prefix[:, columns(width, pair)].T
        halves = []
        for head in (0, 1):
            first, second, extra, inverse = probs[2 * pair + head]
            place = seq * HEADS + 2 * pair + head
            top[place] = first
            bottom[place] = second
            side[place] = extra
            norms[pl.ds(place, 1), :] = inverse
            whole = jnp.concatenate([first, jnp.concatenate([empty, second], axis=1)], axis=0)
            mine = slice(head * (PAIR // 2), (head + 1) * (PAIR // 2))
            halves.append(
                (dot(values[mine], whole) + dot(prefix_values[mine], extra)) * inverse
            )
        attended[rows, columns(0, pair)] = jnp.concatenate(halves, axis=0).astype(BF16).T


def attention_backward(
    seq, width, packed, prefix, upstream, attended, top, bottom, side, norms, prefix_grad
):
    rows = pl.ds(pl.multiple_of(seq * SEQ_LEN, SEQ_LEN), SEQ_LEN)
    pairs = width // PAIR
    lanes = head_lanes()
    head_row = lax.broadcasted_iota(jnp.int32, (8, PAIR), 0)
    head_lane = lax.broadcasted_iota(jnp.int32, (8, PAIR), 1)
    picker = jnp.where(head_lane // (PAIR // 2) == head_row, 1.0, 0.0).astype(BF16)
    empty = jnp.zeros((HALF, HALF), BF16)
    incoming, deltas = [], []
    for pair in range(pairs):
        grad = upstream[rows, columns(0, pair)]
        deltas.append(dot(picker, grad * attended[rows, columns(0, pair)], NT))
        incoming.append(
            pair_products(
                packed[rows, columns(2 * width, pair)], prefix[:, columns(width, pair)], grad, lanes
            )
        )
    slopes, probs = [], []
    for pair in range(pairs):
        for head in (0, 1):
            place = seq * HEADS + 2 * pair + head
            first, second, extra = incoming[pair][head]
            delta = deltas[pair][head : head + 1, :]
            inverse = norms[pl.ds(place, 1), :]
            chances = [
                top[place].astype(F32) * inverse,
                bottom[place].astype(F32) * inverse[:, HALF:],
                side[place].astype(F32) * inverse,
            ]
            first = (chances[0] * (first - delta)).astype(BF16)
            second = (chances[1] * (second - delta[:, HALF:])).astype(BF16)
            extra = (chances[2] * (extra - delta)).astype(BF16)
            slopes.append((first, second, extra))
            probs.append([part.astype(BF16) for part in chances])
    for pair in range(pairs):
        grad = upstream[rows, columns(0, pair)]
        queries = packed[rows, columns(0, pair)]
        keys = packed[rows, columns(width, pair)].T
        prefix_keys = prefix[:, columns(0, pair)].T

        def pulled(stream, first, second, extra):
            masked = [jnp.where(mine, stream, 0) for mine in lanes]
            both = jnp.concatenate(masked, axis=0)
            late = jnp.concatenate([part[HALF:] for part in masked], axis=0)
            joined = [jnp.concatenate(part, axis=1) for part in (first, second)]
            beside = dot(jnp.concatenate(extra, axis=0), stream)
            beside = jnp.where(lanes[0], beside[:PAD], beside[PAD:])
            return dot(joined[0], both), dot(joined[1], late), beside

        left, right = slopes[2 * pair], slopes[2 * pair + 1]
        key_first, key_second, key_extra = pulled(
            queries, (left[0], right[0]), (left[1], right[1]), (left[2], right[2])
        )
        value_first, value_second, value_extra = pulled(
            grad,
            *zip(probs[2 * pair], probs[2 * pair + 1]),
        )
        halves = []
        for head in (0, 1):
            first, second, extra = slopes[2 * pair + head]
            whole = jnp.concatenate([first, jnp.concatenate([empty, second], axis=1)], axis=0)
            mine = slice(head * (PAIR // 2), (head + 1) * (PAIR // 2))
            halves.append(dot(keys[mine], whole) + dot(prefix_keys[mine], extra))
        prefix_grad[:, columns(0, pair)] += key_extra
        prefix_grad[:, columns(width, pair)] += value_extra
        packed[rows, columns(0, pair)] = (
            (jnp.concatenate(halves, axis=0) * 0.125).astype(BF16).T
        )
        packed[rows, columns(width, pair)] = jnp.concatenate(
            [key_first, key_second], axis=0
        ).astype(BF16)
        packed[rows, columns(2 * width, pair)] = jnp.concatenate(
            [value_first, value_second], axis=0
        ).astype(BF16)


def layer_kernel(
    dp_size,
    col_size,
    tokens_hbm,
    cotangent_hbm,
    qkv_hbm,
    out_hbm,
    fc_hbm,
    proj_hbm,
    first_hbm,
    second_hbm,
    ln1_gain,
    ln1_shift,
    qkv_bias,
    out_bias,
    ln2_gain,
    ln2_shift,
    fc_bias,
    proj_bias,
    embedding,
    first_bias,
    second_bias,
    attended,
    stream,
    hidden_out,
    owned_out,
    pre_out,
    embed_out,
    wide,
    out_weight,
    fc_weight,
    proj_weight,
    packed,
    top,
    bottom,
    side,
    norms,
    middle,
    normed,
    activated,
    second_weight,
    prefix,
    prefix_grad,
    padded,
    ff_bias,
    parts_col,
    parts_dp,
    parts_hidden,
    load_sem,
    gather_send,
    gather_recv,
    scatter_send,
    scatter_recv,
    reduce_send,
    reduce_recv,
    hidden_send,
    hidden_recv,
):
    row_count, width = stream.shape
    ff = activated.shape[1]
    tokens = wide.at[pl.ds(0, row_count), pl.ds(3 * width, width)]
    hidden_width = second_weight.shape[0]
    owned = second_weight.shape[1]
    seqs = row_count // SEQ_LEN
    my_dp = lax.axis_index("dp")
    my_col = lax.axis_index("col")

    def col_peer(step):
        return (my_dp, lax.rem(my_col + step, col_size))

    def dp_peer(step):
        return (lax.rem(my_dp + step, dp_size), my_col)

    barrier = pltpu.get_barrier_semaphore()
    for step in range(1, col_size):
        pl.semaphore_signal(barrier, inc=1, device_id=col_peer(step), device_id_type=MESH)
    for step in range(1, dp_size):
        pl.semaphore_signal(barrier, inc=1, device_id=dp_peer(step), device_id_type=MESH)

    first_weight = activated.at[pl.ds(0, width), pl.ds(0, hidden_width)]
    thirds = [pl.ds(third * width, width) for third in range(3)]
    qkv_weight = [wide.at[pl.ds(0, width), third] for third in thirds]
    blocks = row_count // BLOCK
    block_rows = [pl.ds(block * BLOCK, BLOCK) for block in range(blocks)]
    loads = [
        pltpu.make_async_copy(source, target, load_sem.at[place])
        for place, (source, target) in enumerate(
            [(tokens_hbm.at[rows, :], tokens.at[rows, :]) for rows in block_rows]
            + [(first_hbm, first_weight), (second_hbm, second_weight)]
            + [(qkv_hbm.at[:, thirds[third]], qkv_weight[third]) for third in range(3)]
            + [
                (out_hbm, out_weight),
                (fc_hbm, fc_weight),
                (proj_hbm, proj_weight),
                (cotangent_hbm, stream),
            ]
        )
    ]
    for load in loads:
        load.start()
    token_loads, loads = loads[:blocks], loads[blocks:]

    padded[...] = jnp.zeros_like(padded)
    padded[0:PREFIX, :] = embedding[...].astype(F32)
    ff_bias[...] = row(fc_bias)

    gain_one, shift_one = row(ln1_gain), row(ln1_shift)
    for load, rows in zip(token_loads, block_rows):
        load.wait()
        unit = normalise(tokens[rows, :].astype(F32))
        normed[rows, :] = (unit * gain_one + shift_one).astype(BF16)

    loads[0].wait()
    loads[1].wait()
    embed_out[...] = padded[...].astype(BF16)
    pre_hidden = dot(embed_out[...], first_weight[...]) + row(first_bias)
    hidden_full = jnp.tanh(pre_hidden)
    hidden_low = hidden_full.astype(BF16)
    hidden_out[...] = hidden_low
    owned_kv = dot(hidden_low, second_weight[...]) + row(second_bias)
    mine = pl.ds(pl.multiple_of(my_col * owned, PAIR), owned)
    prefix[:, mine] = owned_kv.astype(BF16)
    gathers = [
        pltpu.make_async_remote_copy(
            src_ref=prefix.at[:, mine],
            dst_ref=prefix.at[:, mine],
            send_sem=gather_send.at[step - 1],
            recv_sem=gather_recv.at[step - 1],
            device_id=col_peer(step),
            device_id_type=MESH,
        )
        for step in range(1, col_size)
    ]

    for third in range(3):
        loads[2 + third].wait()
        bias = qkv_bias[pl.ds(third * width, width)].astype(F32).reshape(1, -1)
        part = (dot(normed[...], qkv_weight[third][...]) + bias).astype(BF16)
        packed[:, thirds[third]] = part * BF16(0.125) if third == 0 else part
        if third == 0:
            pl.semaphore_wait(barrier, col_size + dp_size - 2)
            for gather in gathers:
                gather.start()

    for gather in gathers:
        gather.wait()

    def forward_step(seq, carry):
        attention_forward(seq, width, packed, prefix, attended, top, bottom, side, norms)
        return carry

    lax.fori_loop(0, seqs, forward_step, 0)

    loads[5].wait()
    bias = row(out_bias)
    gain_two, shift_two = row(ln2_gain), row(ln2_shift)

    def output_rows(block, rows):
        total = tokens[rows, :].astype(F32) + dot(attended[rows, :], out_weight[...]) + bias
        middle[rows, :] = total.astype(BF16)
        unit = normalise(total)
        normed[rows, :] = (unit * gain_two + shift_two).astype(BF16)

    over_rows(row_count, 4, output_rows)

    for load in loads[6:]:
        load.wait()

    def ff_step(chunk, carry):
        units = pl.ds(pl.multiple_of(chunk * FF_CHUNK, FF_CHUNK), FF_CHUNK)
        bias = ff_bias[:, units]
        for start in range(0, row_count, FF_ROWS):
            rows = pl.ds(start, FF_ROWS)
            pre_act = dot(normed[rows, :], fc_weight[:, units]) + bias
            upstream = dot(stream[rows, :], proj_weight[units, :], NT)
            value, slope = gelu_and_slope(pre_act)
            activated[rows, units] = value.astype(BF16)
            wide[rows, units] = (slope * upstream).astype(BF16)
        return carry

    lax.fori_loop(0, ff // FF_CHUNK, ff_step, 0)

    def middle_rows(block, rows):
        upstream = dot(wide[rows, :], fc_weight[...], NT)
        total = stream[rows, :].astype(F32) + norm_pull(
            middle[rows, :].astype(F32), gain_two, upstream
        )
        low = total.astype(BF16)
        stream[rows, :] = low
        normed[rows, :] = dot(low, out_weight[...], NT).astype(BF16)

    over_rows(row_count, 4, middle_rows)

    reloads = [
        pltpu.make_async_copy(source, target, load_sem.at[place])
        for place, (source, target) in enumerate(
            [(tokens_hbm, tokens)]
            + [(qkv_hbm.at[:, thirds[third]], qkv_weight[third]) for third in range(3)]
        )
    ]
    for load in reloads:
        load.start()

    prefix_grad[...] = jnp.zeros_like(prefix_grad)

    def backward_step(seq, carry):
        attention_backward(
            seq, width, packed, prefix, normed, attended, top, bottom, side, norms, prefix_grad
        )
        return carry

    lax.fori_loop(0, seqs, backward_step, 0)

    scatters = [
        pltpu.make_async_remote_copy(
            src_ref=prefix_grad.at[
                :, pl.ds(pl.multiple_of(lax.rem(my_col + step, col_size) * owned, PAIR), owned)
            ],
            dst_ref=parts_col.at[step - 1],
            send_sem=scatter_send.at[step - 1],
            recv_sem=scatter_recv.at[step - 1],
            device_id=col_peer(step),
            device_id_type=MESH,
        )
        for step in range(1, col_size)
    ]
    reduces = [
        pltpu.make_async_remote_copy(
            src_ref=parts_dp.at[my_dp],
            dst_ref=parts_dp.at[my_dp],
            send_sem=reduce_send.at[step - 1],
            recv_sem=reduce_recv.at[step - 1],
            device_id=dp_peer(step),
            device_id_type=MESH,
        )
        for step in range(1, dp_size)
    ]
    hiddens = [
        pltpu.make_async_remote_copy(
            src_ref=parts_hidden.at[my_col],
            dst_ref=parts_hidden.at[my_col],
            send_sem=hidden_send.at[step - 1],
            recv_sem=hidden_recv.at[step - 1],
            device_id=col_peer(step),
            device_id_type=MESH,
        )
        for step in range(1, col_size)
    ]

    def exchange(stage):
        if stage == 0:
            for scatter in scatters:
                scatter.start()
        elif stage == 1:
            for scatter in scatters:
                scatter.wait()
            total = prefix_grad[:, mine]
            for step in range(1, col_size):
                total = total + parts_col[step - 1]
            parts_dp[my_dp] = total
            for reduce in reduces:
                reduce.start()
        elif stage == 2:
            for reduce in reduces:
                reduce.wait()
            total = parts_dp[0]
            for step in range(1, dp_size):
                total = total + parts_dp[step]
            low = total.astype(BF16)
            owned_out[...] = low
            parts_hidden[my_col] = dot(low, second_weight[...], NT)
            for part in hiddens:
                part.start()
        else:
            for part in hiddens:
                part.wait()
            total = parts_hidden[0]
            for step in range(1, col_size):
                total = total + parts_hidden[step]
            first_weight_sum = hidden_full * hidden_full
            pre_out[...] = (total * (1.0 - first_weight_sum)).astype(BF16)

    exchange(0)
    proj_row = row(proj_bias)

    def proj_rows(block, rows):
        total = middle[rows, :].astype(F32) + dot(activated[rows, :], proj_weight[...]) + proj_row
        attended[rows, :] = total.astype(BF16)
        pl.when(block == 1)(lambda: exchange(1))

    over_rows(row_count, 2, proj_rows)
    for load in reloads:
        load.wait()

    def grad_rows(block, rows):
        upstream = dot(packed[rows, :], wide[0:width, 0 : 3 * width], NT)
        total = stream[rows, :].astype(F32) + norm_pull(
            tokens[rows, :].astype(F32), gain_one, upstream
        )
        stream[rows, :] = total.astype(BF16)
        pl.when(block == 1)(lambda: exchange(2))

    over_rows(row_count, 2, grad_rows)
    exchange(3)

def small_kernel(
    block_in,
    grad_in,
    hidden,
    owned,
    pre,
    embedding,
    first_hbm,
    block_out,
    grad_out,
    embed_out,
    first_out,
    first_bias_out,
    second_out,
    second_bias_out,
    first_weight,
    first_grad,
    second_grad,
    first_bias_grad,
    second_bias_grad,
    embed_grad,
    sem,
):
    load = pltpu.make_async_copy(first_hbm, first_weight, sem.at[0])
    writes = [
        pltpu.make_async_copy(source, target, sem.at[1 + place])
        for place, (source, target) in enumerate(
            [
                (block_in, block_out),
                (grad_in, grad_out),
                (second_grad, second_out),
                (first_grad, first_out),
                (first_bias_grad, first_bias_out),
                (second_bias_grad, second_bias_out),
                (embed_grad, embed_out),
            ]
        )
    ]
    load.start()
    writes[0].start()
    writes[1].start()
    second_grad[...] = dot(hidden[...], owned[...], TN)
    writes[2].start()
    first_grad[...] = dot(embedding[...], pre[...], TN)
    writes[3].start()
    first_bias_grad[...] = jnp.sum(pre[...].astype(F32), axis=0)
    writes[4].start()
    second_bias_grad[...] = jnp.sum(owned[...].astype(F32), axis=0)
    writes[5].start()
    load.wait()
    embed_grad[...] = dot(pre[...], first_weight[...], NT)[:PREFIX]
    writes[6].start()
    for write in writes:
        write.wait()


def shards(
    dp_size,
    col_size,
    tokens,
    cotangent,
    ln1_gain,
    ln1_shift,
    qkv_weight,
    qkv_bias,
    out_weight,
    out_bias,
    ln2_gain,
    ln2_shift,
    fc_weight,
    fc_bias,
    proj_weight,
    proj_bias,
    embedding,
    first_weight,
    first_bias,
    second_weight,
    second_bias,
):
    row_count, width = tokens.shape
    ff = fc_weight.shape[1]
    hidden_width, owned = second_weight.shape
    heads = row_count // SEQ_LEN * HEADS
    anywhere = pl.BlockSpec(memory_space=pl.ANY)
    local = pl.BlockSpec(memory_space=pltpu.VMEM)
    dma = pltpu.SemaphoreType.DMA
    results = pl.pallas_call(
        functools.partial(layer_kernel, dp_size, col_size),
        out_shape=(
            pltpu.VMEM((row_count, width), BF16),
            pltpu.VMEM((row_count, width), BF16),
            pltpu.VMEM((PAD, hidden_width), BF16),
            pltpu.VMEM((PAD, owned), BF16),
            pltpu.VMEM((PAD, hidden_width), BF16),
            pltpu.VMEM((PAD, width), BF16),
        ),
        in_specs=[anywhere] * 8 + [local] * 11,
        out_specs=[local] * 6,
        scratch_shapes=[
            pltpu.VMEM((max(row_count, width), ff), BF16),
            pltpu.VMEM((width, width), BF16),
            pltpu.VMEM((width, ff), BF16),
            pltpu.VMEM((ff, width), BF16),
            pltpu.VMEM((row_count, 3 * width), BF16),
            pltpu.VMEM((heads, HALF, SEQ_LEN), BF16),
            pltpu.VMEM((heads, HALF, HALF), BF16),
            pltpu.VMEM((heads, PAD, SEQ_LEN), BF16),
            pltpu.VMEM((heads, SEQ_LEN), F32),
            pltpu.VMEM((row_count, width), BF16),
            pltpu.VMEM((row_count, width), BF16),
            pltpu.VMEM((max(row_count, width), ff), BF16),
            pltpu.VMEM((hidden_width, owned), BF16),
            pltpu.VMEM((PAD, col_size * owned), BF16),
            pltpu.VMEM((PAD, col_size * owned), F32),
            pltpu.VMEM((PAD, width), F32),
            pltpu.VMEM((1, ff), F32),
            pltpu.VMEM((col_size - 1, PAD, owned), F32),
            pltpu.VMEM((dp_size, PAD, owned), F32),
            pltpu.VMEM((col_size, PAD, hidden_width), F32),
            dma((9 + row_count // BLOCK,)),
            dma((col_size - 1,)),
            dma((col_size - 1,)),
            dma((col_size - 1,)),
            dma((col_size - 1,)),
            dma((dp_size - 1,)),
            dma((dp_size - 1,)),
            dma((col_size - 1,)),
            dma((col_size - 1,)),
        ],
        compiler_params=pltpu.CompilerParams(
            collective_id=0, has_side_effects=True, vmem_limit_bytes=239 * 2**18
        ),
        name="layer",
    )(
        tokens,
        cotangent,
        qkv_weight,
        out_weight,
        fc_weight,
        proj_weight,
        first_weight,
        second_weight,
        ln1_gain,
        ln1_shift,
        qkv_bias,
        out_bias,
        ln2_gain,
        ln2_shift,
        fc_bias,
        proj_bias,
        embedding,
        first_bias,
        second_bias,
    )
    held = [pltpu.with_memory_space_constraint(result, pltpu.VMEM) for result in results]
    return pl.pallas_call(
        small_kernel,
        out_shape=(
            jax.ShapeDtypeStruct((row_count, width), BF16),
            jax.ShapeDtypeStruct((row_count, width), BF16),
            jax.ShapeDtypeStruct((PREFIX, width), F32),
            jax.ShapeDtypeStruct((width, hidden_width), F32),
            jax.ShapeDtypeStruct((hidden_width,), F32),
            jax.ShapeDtypeStruct((hidden_width, owned), F32),
            jax.ShapeDtypeStruct((owned,), F32),
        ),
        in_specs=[local] * 6 + [anywhere],
        out_specs=[anywhere] * 7,
        scratch_shapes=[
            pltpu.VMEM((width, hidden_width), BF16),
            pltpu.VMEM((width, hidden_width), F32),
            pltpu.VMEM((hidden_width, owned), F32),
            pltpu.VMEM((hidden_width,), F32),
            pltpu.VMEM((owned,), F32),
            pltpu.VMEM((PREFIX, width), F32),
            dma((8,)),
        ],
        compiler_params=pltpu.CompilerParams(vmem_limit_bytes=16 * 2**20),
        name="small_grads",
    )(*held, first_weight)


def solution(mesh):
    placed = (
        P(("dp", "col"), None),
        P(("dp", "col"), None),
        P(),
        P(),
        P(),
        P(),
        P(),
        P(),
        P(),
        P(),
        P(),
        P(),
        P(),
        P(),
        P(),
        P(),
        P(),
        P(None, "col"),
        P("col"),
    )
    return jax.shard_map(
        functools.partial(shards, mesh.shape["dp"], mesh.shape["col"]),
        mesh=mesh,
        in_specs=placed,
        out_specs=(
            P(("dp", "col"), None),
            P(("dp", "col"), None),
            P(),
            P(),
            P(),
            P(None, "col"),
            P("col"),
        ),
        check_vma=False,
    )
```
